256 devices in a mesh: ctx: 32 (over z, y_hi, core), exp: 8 (over y_lo, x).
Axes of the slice: x: 4, y: 4 (y_hi: 2, y_lo: 2; y = y_hi * 2 + y_lo), z: 8, core: 2. Of those that a mesh axis runs over, the one named last changes fastest.
Arguments:
- residual: bfloat16 [16384, 2048], P('ctx', 'exp'), may hold values from -6 to 6
- query_vectors: bfloat16 [16384, 2048], P('ctx', 'exp'), may hold values from -10 to 10
- key_vectors: bfloat16 [16384, 2048], P('ctx', 'exp'), may hold values from -10 to 10
- value_vectors: bfloat16 [16384, 2048], P('ctx', 'exp'), may hold values from -6 to 6
- out_weight: bfloat16 [2048, 2048], P('exp'), may hold values from -0.125 to 0.125
- norm_gain: float32 [2048], replicated, may hold values from 0.25 to 1.75
- species: int32 [2048, 1], P('ctx'), may hold values from 0 to 63; in each aligned block of 64 rows (0 to 63, 64 to 127, ...) at most 2 rows name the same one
- gate_weight: bfloat16 [64, 2048, 2816], P('ctx', None, 'exp'), may hold values from -0.125 to 0.125
- up_weight: bfloat16 [64, 2048, 2816], P('ctx', None, 'exp'), may hold values from -0.125 to 0.125
- down_weight: bfloat16 [64, 2816, 2048], P('ctx', 'exp'), may hold values from -0.109375 to 0.109375
Outputs:
- layer_out: bfloat16 [16384, 2048], P('ctx', 'exp')
The draws below stay inside these ranges and needn't reach their ends.
Inputs may be any that keep to these rules, and one draw needn't show every extreme that they name: Among the 64 blocks of one device (aligned runs of rows of species) no species occurs more than 2 times; every species occurs somewhere.
All inputs are finite; a program needn't handle non-finite values.
Results may differ from the reference program's by a relative error of at most 0.02.
Values may be sent and summed in bfloat16 or wider, within the bound.
A program may use at most 128 MiB of HBM per device.

```python
import math
import jax
import jax.numpy as jnp
import numpy as np
from jax import lax

D = 2048
HEADS = 16
HEAD_DIM = 128
FF = 2816
BLK = 8
MOST = 2
TOK_DEV = 512
SEQ = 16384
NBLK = 2048
EXPERTS = 64
N_CTX = 32
N_EXP = 8


def draw_query_vectors(key, part):
    key = jax.random.fold_in(key, 11)
    width = HEADS * HEAD_DIM
    base = jnp.clip(1.7 * jax.random.normal(key, (SEQ, width), jnp.float32), -10.0, 10.0)
    return base.astype(jnp.bfloat16)


def draw_key_vectors(key, part):
    key = jax.random.fold_in(key, 23)
    width = HEADS * HEAD_DIM
    base = jnp.clip(1.7 * jax.random.normal(key, (SEQ, width), jnp.float32), -10.0, 10.0)
    return base.astype(jnp.bfloat16)


def steps_of(stream_key, shape, pieces, least, high):
    gain = 1.0
    for dim, blocks in pieces:
        steps = jax.random.uniform(jax.random.fold_in(jax.random.fold_in(stream_key, 6), dim), (blocks,), jnp.float32, least / len(pieces), high / len(pieces))
        gain = gain * jnp.repeat(jnp.exp(steps), shape[dim] // blocks).reshape((-1,) + (1,) * (len(shape) - 1 - dim))
    return gain


def shared_out(own_key, own, number, rows, number_of, top, limit, skew):
    sequence = jax.random.permutation(own_key, number_of)
    packed, usual = shares(number_of, rows * top, limit, skew, True), shares(number_of, rows * top, limit, skew, False)
    places = jnp.arange(number_of)

    def named(tallies, turn):
        used = int((tallies > 0).sum())
        fixed = max(1, used // 4)
        moved = fixed + (places - fixed + turn * (used - fixed)) % max(1, number_of - fixed)
        return jnp.zeros((number_of,), jnp.int32).at[sequence[jnp.where(places < fixed, places, moved)]].set(jnp.asarray(tallies, jnp.int32))

    tallies = jnp.where(number % 4 == 0, named(packed, number // 4), named(usual, number - number // 4 - 1))
    mixed = jax.random.permutation(jax.random.fold_in(own, 3), number_of)
    giver, taker = mixed[0:number_of // 2 * 2:2], mixed[1:number_of // 2 * 2:2]
    margin = jnp.minimum(tallies[giver] - 1, limit - tallies[taker]) // 2
    margin = jnp.where((giver == sequence[0]) | (taker == sequence[0]) | (tallies[taker] == 0), 0, jnp.maximum(margin, 0))
    moved = jax.random.randint(jax.random.fold_in(own, 4), (number_of // 2,), 0, 1 << 20) % (margin + 1)
    tallies = tallies.at[giver].add(-moved).at[taker].add(moved)
    members = jnp.searchsorted(jnp.cumsum(tallies), jnp.arange(rows * top), side="right").astype(jnp.int32)
    grid = members.reshape(top, rows).T
    grid = grid[jax.random.permutation(jax.random.fold_in(own, 1), rows)]
    turn = jax.random.randint(jax.random.fold_in(own, 2), (rows, 1), 0, top)
    return jnp.take_along_axis(grid, (jnp.arange(top)[None, :] + turn) % top, axis=1)


def shares(count, total, reach, slope, full):
    weights = [(1 << 20) // math.isqrt(grade ** slope) + 1 for grade in range(1, count + 1)]
    largest = reach if full else min(reach, max(-(-total // count), total * weights[0] // sum(weights)))
    least = 1 if total - largest >= count - 1 else 0
    holding, rest = [largest] + [least] * (count - 1), total - largest - least * (count - 1)
    while rest > 0:
        movable = [i for i in range(1, count) if holding[i] < largest] or [i for i in range(1, count) if holding[i] < reach]
        mass, budget = sum([weights[i] for i in movable]), rest
        for i in movable:
            addition = min(reach - holding[i], max(1, budget * weights[i] // mass), rest)
            holding[i] = holding[i] + addition
            rest = rest - addition
    return np.array(holding)


def noise(rng, shape, deviation, most, split=(), kind=jnp.bfloat16):
    gain = steps_of(rng, shape, split, -0.22, 0.18) if split else 1.0
    values = jax.random.normal(rng, shape, jnp.float32) * deviation * gain
    return jnp.minimum(jnp.maximum(values, -most), most).astype(kind)


def setup_inputs(seed: int = 0) -> dict:
    keys = jax.random.split(jax.random.key(seed), 11)
    residual = noise(keys[0], (SEQ, D), 1.0, 6.0, ((0, 32), (1, 8)))
    query_vectors = draw_query_vectors(jax.random.fold_in(keys[10], 71), 0)
    key_vectors = draw_key_vectors(jax.random.fold_in(keys[10], 71), 0)
    value_vectors = noise(keys[3], (SEQ, HEADS * HEAD_DIM), 1.0, 6.0, ((0, 32), (1, 8)))
    out_weight = noise(keys[4], (HEADS * HEAD_DIM, D), (HEADS * HEAD_DIM) ** -0.5, 0.125, ((0, 8),))
    norm_gain = jnp.clip(1.0 + 0.15 * jax.random.normal(keys[5], (D,), jnp.float32), 0.25, 1.75)
    species_keys = jax.random.split(jax.random.fold_in(keys[6], 1), NBLK // (TOK_DEV // BLK))
    species_turns = jax.random.permutation(jax.random.fold_in(keys[6], 3), NBLK // (TOK_DEV // BLK))
    species = jax.vmap(lambda own, number: shared_out(jax.random.fold_in(keys[6], 2), own, number, TOK_DEV // BLK, EXPERTS, 1, MOST, 2))(species_keys, species_turns).reshape((NBLK, 1))
    gate_weight = noise(keys[7], (EXPERTS, D, FF), D ** -0.5, 0.125, ((0, 32), (2, 8)))
    up_weight = noise(keys[8], (EXPERTS, D, FF), D ** -0.5, 0.125, ((0, 32), (2, 8)))
    down_weight = noise(keys[9], (EXPERTS, FF, D), FF ** -0.5, 0.109375, ((0, 32), (1, 8)))
    return {"residual": residual, "query_vectors": query_vectors, "key_vectors": key_vectors, "value_vectors": value_vectors, "out_weight": out_weight, "norm_gain": norm_gain, "species": species, "gate_weight": gate_weight, "up_weight": up_weight, "down_weight": down_weight}


EPSILON = 1e-06

def head_attention(operands):
    query_head, key_head, value_head = operands
    block_len = math.gcd(SEQ, 2048)
    factor = 1.0 / math.sqrt(HEAD_DIM)

    def one_block(query_block):
        scores = jnp.dot(query_block, key_head.T, preferred_element_type=jnp.float32) * factor
        weights = jnp.exp(scores - lax.optimization_barrier(jnp.max(scores, axis=-1, keepdims=True)))
        denom_sum = lax.optimization_barrier(jnp.sum(weights, axis=-1, keepdims=True))
        mixed = jnp.dot(weights.astype(jnp.bfloat16), value_head, preferred_element_type=jnp.float32)
        return mixed / denom_sum
    blocks = query_head.reshape(SEQ // block_len, block_len, HEAD_DIM)
    return lax.map(one_block, blocks).reshape(SEQ, HEAD_DIM)

def split_heads(vectors):
    return vectors.reshape(SEQ, HEADS, HEAD_DIM).transpose(1, 0, 2)

def expert_rows(tokens_in, gate_mat, up_mat, down_mat):
    gate = jnp.dot(tokens_in, gate_mat, preferred_element_type=jnp.float32)
    lifted = jnp.dot(tokens_in, up_mat, preferred_element_type=jnp.float32)
    hidden = (jax.nn.silu(gate) * lifted).astype(jnp.bfloat16)
    groups = hidden.reshape(tokens_in.shape[0], N_EXP, FF // N_EXP).astype(jnp.float32)
    down_groups = down_mat.reshape(N_EXP, FF // N_EXP, D).astype(jnp.float32)
    parts = jnp.einsum('rgf,gfd->grd', groups, down_groups, precision=lax.Precision.HIGHEST)
    rounded = lax.optimization_barrier(parts.astype(jnp.bfloat16))
    return lax.optimization_barrier(jnp.sum(rounded.astype(jnp.float32), axis=0)).astype(jnp.bfloat16)

def reference(residual, query_vectors, key_vectors, value_vectors, out_weight, norm_gain, species, gate_weight, up_weight, down_weight):
    heads_out = lax.map(head_attention, (split_heads(query_vectors), split_heads(key_vectors), split_heads(value_vectors)))
    attended = heads_out.transpose(1, 0, 2).reshape(SEQ, HEADS * HEAD_DIM).astype(jnp.bfloat16)
    mixed_sum = jnp.dot(attended, out_weight, preferred_element_type=jnp.float32)
    stream = (residual.astype(jnp.float32) + mixed_sum).astype(jnp.bfloat16)
    stream32 = stream.astype(jnp.float32)
    mean_sq = lax.optimization_barrier(jnp.mean(stream32 * stream32, axis=-1, keepdims=True))
    normed = (stream32 * lax.rsqrt(mean_sq + EPSILON) * norm_gain).astype(jnp.bfloat16)
    block_ids = species[:, 0].astype(jnp.int32)
    padded = jnp.concatenate([normed.reshape(NBLK, BLK * D), jnp.zeros((1, BLK * D), normed.dtype)], axis=0)

    def one_expert(collected, inputs):
        gate_mat, up_mat, down_mat, ident = inputs
        picks = jnp.nonzero(block_ids == ident, size=N_CTX * MOST, fill_value=NBLK)[0].astype(jnp.int32)
        chosen = padded[picks].reshape(N_CTX * MOST * BLK, D)
        result = expert_rows(chosen, gate_mat, up_mat, down_mat).reshape(N_CTX * MOST, BLK * D)
        return (collected.at[picks].add(result.astype(jnp.float32)), None)
    start_sum = jnp.zeros((NBLK + 1, BLK * D), jnp.float32)
    collected, unused = lax.scan(one_expert, start_sum, (gate_weight, up_weight, down_weight, jnp.arange(EXPERTS, dtype=jnp.int32)))
    expert_out = collected[:NBLK].reshape(SEQ, D)
    return (stream32 + expert_out).astype(jnp.bfloat16)
```

```python
import functools
import math

import jax
import jax.numpy as jnp
from jax import lax
from jax.experimental import pallas as pl
from jax.experimental.pallas import tpu as pltpu
from jax.sharding import PartitionSpec as P

HEAD_DIM = 128
BLK = 8
MOST = 2
EPSILON = 1e-06
EXP2_FACTOR = math.log2(math.e) / math.sqrt(HEAD_DIM)
VMEM_BYTES = 60 * 1024 * 1024
TILE_Q = 256
Z_CHUNKS = ((0, 1), (7, 2), (6, 3), (5, 4))
CHUNKS = len(Z_CHUNKS)
MESH = pl.DeviceIdType.MESH


def remote(src, dst, send_sem, recv_sem, where):
    return pltpu.make_async_remote_copy(
        src_ref=src,
        dst_ref=dst,
        send_sem=send_sem,
        recv_sem=recv_sem,
        device_id=where,
        device_id_type=MESH,
    )


def meet(others):
    barrier = pltpu.get_barrier_semaphore()
    for where in others:
        pl.semaphore_signal(barrier, inc=1, device_id=where, device_id_type=MESH)
    pl.semaphore_wait(barrier, len(others))


def attention_kernel(
    q_ref, k_ref, v_ref, o_ref,
    qbuf, kv, acc, top, o_send, o_recv, l_send, l_recv,
    r_ss, r_rs, l_ss, l_rs, s_ss, s_rs, x_ss, x_rs,
):
    ctx = lax.axis_index("ctx")
    z, lane = ctx // 4, ctx % 4
    right = {"ctx": ((z + 1) % 8) * 4 + lane}
    left = {"ctx": ((z + 7) % 8) * 4 + lane}
    sibling = {"ctx": z * 4 + (lane // 2) * 2 + (lane + 1) % 2}
    partner = {"ctx": z * 4 + (lane + 2) % 4}

    half = 256
    for h in range(2):
        kv[0, 0, h, 0] = k_ref[h * half : (h + 1) * half, :]
        kv[0, 0, h, 1] = v_ref[h * half : (h + 1) * half, :]
    qbuf[0] = q_ref[...]
    meet((right, left, sibling, partner))

    def right_copy(t):
        return remote(
            kv.at[0, t // 2, t % 2], kv.at[0, 1 + t // 2, t % 2], r_ss.at[t], r_rs.at[t], right
        )

    def left_copy(t):
        return remote(
            kv.at[0, (8 - t // 2) % 8, 1 - t % 2],
            kv.at[0, 7 - t // 2, 1 - t % 2],
            l_ss.at[t],
            l_rs.at[t],
            left,
        )

    def places(t):
        return ((1 + t // 2, t % 2), (7 - t // 2, 1 - t % 2))

    def sibling_copy(way, t):
        slot, part = places(t)[way]
        return remote(
            kv.at[0, slot, part], kv.at[1, slot, part], s_ss.at[way, t], s_rs.at[way, t], sibling
        )

    query_copy = remote(qbuf.at[0], qbuf.at[1], x_ss.at[0], x_rs.at[0], partner)
    own_copy = remote(kv.at[0, 0], kv.at[1, 0], x_ss.at[1], x_rs.at[1], sibling)
    right_copy(0).start()
    left_copy(0).start()
    query_copy.start()
    own_copy.start()
    right_copy(1).start()
    left_copy(1).start()

    acc[...] = jnp.zeros_like(acc)
    top[...] = jnp.full_like(top, -1e30)
    ones = jnp.ones((half, HEAD_DIM), jnp.bfloat16)

    def attend(queries, kind, pair):
        def tile(index, unused):
            rows = pl.ds(pl.multiple_of(index * TILE_Q, TILE_Q), TILE_Q)
            for head in range(2):
                cols = slice(head * HEAD_DIM, (head + 1) * HEAD_DIM)
                q = qbuf[queries, rows, cols]
                scores = [
                    lax.dot_general(
                        q,
                        kv[kind, slot, part, 0, :, cols],
                        (((1,), (1,)), ((), ())),
                        preferred_element_type=jnp.float32,
                    )
                    for slot, part in pair
                ]
                before = top[queries, head, rows, :]
                best = jnp.max(jnp.maximum(scores[0], scores[1]), axis=1, keepdims=True)
                now = jnp.maximum(before, best)
                top[queries, head, rows, :] = now
                now2 = jnp.concatenate([now, now], axis=1)
                total = None
                for s, (slot, part) in zip(scores, pair):
                    weights = jnp.exp2((s - now2) * EXP2_FACTOR).astype(jnp.bfloat16)
                    wide = jnp.concatenate([kv[kind, slot, part, 1, :, cols], ones], axis=1)
                    term = jnp.dot(weights, wide, preferred_element_type=jnp.float32)
                    total = term if total is None else total + term
                shrink = jnp.exp2((before - now) * EXP2_FACTOR)
                shrink2 = jnp.concatenate([shrink, shrink], axis=1)
                acc[queries, head, rows, :] = acc[queries, head, rows, :] * shrink2 + total
            return unused

        lax.fori_loop(0, 512 // TILE_Q, tile, 0)

    own_pair = ((0, 0), (0, 1))
    attend(0, 0, own_pair)
    query_copy.wait_recv()
    attend(1, 0, own_pair)
    own_copy.wait_recv()
    attend(0, 1, own_pair)
    attend(1, 1, own_pair)

    def stage(t, unused):
        right_copy(t).wait_recv()

        @pl.when(t < 5)
        def _():
            right_copy(t + 2).start()

        sibling_copy(0, t).start()
        left_copy(t).wait_recv()

        @pl.when(t < 5)
        def _():
            left_copy(t + 2).start()

        sibling_copy(1, t).start()

        def both(queries, more):
            attend(queries, 0, places(t))
            return more

        lax.fori_loop(0, 2, both, 0)
        sibling_copy(0, t).wait_recv()
        sibling_copy(1, t).wait_recv()

        def both_more(queries, more):
            attend(queries, 1, places(t))
            return more

        lax.fori_loop(0, 2, both_more, 0)
        return unused

    lax.fori_loop(0, 7, stage, 0)

    for head in range(2):
        cols = slice(head * HEAD_DIM, (head + 1) * HEAD_DIM)
        denom = acc[1, head, :, HEAD_DIM:]
        o_send[:, cols] = (acc[1, head, :, :HEAD_DIM] / denom).astype(jnp.bfloat16)
        level = top[1, head] * EXP2_FACTOR + jnp.log2(denom)
        l_send[head * 8 : head * 8 + 8, :] = level.T[:8, :]
    out_copy = remote(o_send, o_recv, x_ss.at[2], x_rs.at[2], partner)
    level_copy = remote(l_send, l_recv, x_ss.at[3], x_rs.at[3], partner)
    out_copy.start()
    level_copy.start()

    def drain(t, unused):
        right_copy(t).wait_send()
        left_copy(t).wait_send()
        sibling_copy(0, t).wait_send()
        sibling_copy(1, t).wait_send()
        return unused

    lax.fori_loop(0, 7, drain, 0)
    query_copy.wait_send()
    own_copy.wait_send()
    out_copy.wait()
    level_copy.wait()
    for head in range(2):
        cols = slice(head * HEAD_DIM, (head + 1) * HEAD_DIM)
        denom = acc[0, head, :, HEAD_DIM:]
        mine = acc[0, head, :, :HEAD_DIM] / denom
        level = top[0, head] * EXP2_FACTOR + jnp.log2(denom)
        other = jnp.broadcast_to(l_recv[head * 8 : head * 8 + 1, :], (128, 512)).T
        high = jnp.maximum(level, other)
        w_mine = jnp.exp2(level - high)
        w_other = jnp.exp2(other - high)
        theirs = o_recv[:, cols].astype(jnp.float32)
        o_ref[:, cols] = ((mine * w_mine + theirs * w_other) / (w_mine + w_other)).astype(
            jnp.bfloat16
        )


def attention(q, k, v):
    rows, width = q.shape
    dma = pltpu.SemaphoreType.DMA
    return pl.pallas_call(
        attention_kernel,
        out_shape=jax.ShapeDtypeStruct((rows, width), jnp.bfloat16),
        in_specs=[pl.BlockSpec(memory_space=pltpu.VMEM)] * 3,
        out_specs=pl.BlockSpec(memory_space=pltpu.VMEM),
        scratch_shapes=[
            pltpu.VMEM((2, 512, 256), jnp.bfloat16),
            pltpu.VMEM((2, 8, 2, 2, 256, 256), jnp.bfloat16),
            pltpu.VMEM((2, 2, 512, 256), jnp.float32),
            pltpu.VMEM((2, 2, 512, 128), jnp.float32),
            pltpu.VMEM((512, 256), jnp.bfloat16),
            pltpu.VMEM((512, 256), jnp.bfloat16),
            pltpu.VMEM((16, 512), jnp.float32),
            pltpu.VMEM((16, 512), jnp.float32),
            dma((7,)),
            dma((7,)),
            dma((7,)),
            dma((7,)),
            dma((2, 7)),
            dma((2, 7)),
            dma((4,)),
            dma((4,)),
        ],
        compiler_params=pltpu.CompilerParams(
            collective_id=0, has_side_effects=True, vmem_limit_bytes=VMEM_BYTES
        ),
        cost_estimate=pl.CostEstimate(
            flops=8 * 512 * 16384 * 128, bytes_accessed=2**21, transcendentals=512 * 16384 * 2
        ),
    )(q, k, v)


def f32(value):
    return value.astype(jnp.float32)


def expert_kernel(
    att_ref, wo_ref, res_ref, gain_ref, pack_ref, unpack_ref, gate_hbm, up_hbm, down_hbm, out_ref,
    gate, up, down, stream, packed, agb, normed, back, fin,
    parts1, y1a, p1, h1, t1, y1b,
    parts2, y2a, p2, h2, t2, y2b,
    w_sem, rs1_ss, rs1_rs, rs2_ss, rs2_rs, ag_ss, ag_rs, b_ss, b_rs, f_ss, f_rs,
):
    ctx = lax.axis_index("ctx")
    z, lane = ctx // 4, ctx % 4
    exp = lax.axis_index("exp")
    x, y = exp % 4, exp // 4

    def at(dx, dy):
        return ((y + dy) % 2) * 4 + (x + dx) % 4

    right, left, across = {"exp": at(1, 0)}, {"exp": at(3, 0)}, {"exp": at(0, 1)}

    def ctx_at(dz, dl):
        return ((z + dz) % 8) * 4 + (lane + dl) % 4

    loads = [
        pltpu.make_async_copy(src, dst, w_sem.at[i])
        for i, (src, dst) in enumerate(((gate_hbm, gate), (up_hbm, up), (down_hbm, down)))
    ]
    for load in loads:
        load.start()

    peers = [{"ctx": ctx_at(dz, dl)} for dz in range(8) for dl in range(4) if dz or dl]
    meet([right, left, across] + peers)

    class Reduce:
        def __init__(self, parts, ya, pp, hh, tt, yb, ss, rs):
            self.parts, self.ya, self.pp, self.hh, self.tt, self.yb = parts, ya, pp, hh, tt, yb
            self.ss, self.rs = ss, rs
            self.rows = parts.shape[2]

        def copy(self, c, i):
            parts, mid = self.parts, self.rows // 2
            low, high = pl.ds(0, mid), pl.ds(mid, mid)
            src, dst, where = (
                (parts.at[c, at(2, 1)], self.ya.at[c], across),
                (parts.at[c, at(1, 1)], self.pp.at[c, 0], right),
                (parts.at[c, at(3, 1)], self.pp.at[c, 1], left),
                (parts.at[c, at(2, 0), low], self.hh.at[c, 0], right),
                (parts.at[c, at(2, 0), high], self.hh.at[c, 1], left),
                (parts.at[c, at(1, 0)], self.tt.at[c, 0], right),
                (parts.at[c, at(3, 0)], self.tt.at[c, 1], left),
                (parts.at[c, at(0, 1)], self.yb.at[c], across),
            )[i]
            return remote(src, dst, self.ss.at[c, i], self.rs.at[c, i], where)

        def first(self, c):
            for i in range(3):
                self.copy(c, i).start()

        def second(self, c):
            parts = self.parts
            self.copy(c, 0).wait_recv()
            far = at(2, 0)
            parts[c, far] = (f32(parts[c, far]) + f32(self.ya[c])).astype(jnp.bfloat16)
            self.copy(c, 3).start()
            self.copy(c, 4).start()

        def third(self, c):
            parts, mid = self.parts, self.rows // 2
            self.copy(c, 1).wait_recv()
            self.copy(c, 2).wait_recv()
            other = at(0, 1)
            parts[c, other] = (
                f32(parts[c, other]) + f32(self.pp[c, 0]) + f32(self.pp[c, 1])
            ).astype(jnp.bfloat16)
            self.copy(c, 7).start()
            for way, rows in ((0, pl.ds(0, mid)), (1, pl.ds(mid, mid))):
                self.copy(c, 3 + way).wait_recv()
                near = at(1 if way == 0 else 3, 0)
                parts[c, near, rows] = (
                    f32(parts[c, near, rows]) + f32(self.hh[c, way])
                ).astype(jnp.bfloat16)
                self.copy(c, 5 + way).start()

        def last(self, c):
            for i in (5, 6, 7):
                self.copy(c, i).wait_recv()
            return (f32(self.parts[c, at(0, 0)]) + f32(self.tt[c, 0])) + (
                f32(self.tt[c, 1]) + f32(self.yb[c])
            )

        def drain(self, c):
            for i in range(8):
                self.copy(c, i).wait_send()

    one = Reduce(parts1, y1a, p1, h1, t1, y1b, rs1_ss, rs1_rs)
    for c in range(2):
        rows = slice(c * 256, (c + 1) * 256)
        for f in range(8):
            parts1[c, f] = jnp.dot(
                att_ref[rows, :], wo_ref[:, f * 256 : (f + 1) * 256],
                preferred_element_type=jnp.float32,
            ).astype(jnp.bfloat16)
        one.first(c)
    for c in range(2):
        one.second(c)
    for c in range(2):
        one.third(c)
    for c in range(2):
        rows = slice(c * 256, (c + 1) * 256)
        stream[rows, :] = (f32(res_ref[rows, :]) + one.last(c)).astype(jnp.bfloat16)

    me = at(0, 0)
    slots = [
        [(dz, dl) for dz in pair for dl in range(4)] for pair in Z_CHUNKS
    ]

    def send_copy(c, i):
        dz, dl = slots[c][i]
        to = ctx_at(dz, dl)
        return remote(
            packed.at[to], agb.at[c, me, :, i], b_ss.at[c, i], b_rs.at[c, i], {"ctx": to}
        )

    def back_copy(c, i):
        dz, dl = slots[c][i]
        to = ctx_at(8 - dz, 4 - dl)
        return remote(
            fin.at[c, :, i], back.at[ctx], f_ss.at[c, i], f_rs.at[c, i], {"ctx": to}
        )

    def remote_slots(c):
        return [i for i in range(8) if slots[c][i] != (0, 0)]

    for part in range(4):
        packed[part * 8 : (part + 1) * 8] = jnp.dot(
            pack_ref[part * 256 : (part + 1) * 256, :], stream[...],
            preferred_element_type=jnp.float32,
        ).astype(jnp.bfloat16).reshape(8, 2, 16, 256)
    for c in range(CHUNKS):
        for i in remote_slots(c):
            send_copy(c, i).start()
    agb[0, me, :, 0] = packed[ctx]

    def gather_copy(c, i):
        src, where = (
            (agb.at[c, me], across),
            (agb.at[c, me], right),
            (agb.at[c, me], left),
            (agb.at[c, at(0, 1)], right),
            (agb.at[c, at(0, 1)], left),
            (agb.at[c, at(3, 0), 0], right),
            (agb.at[c, at(1, 0), 1], left),
            (agb.at[c, at(2, 0)], across),
        )[i]
        return remote(src, src, ag_ss.at[c, i], ag_rs.at[c, i], where)

    def gather_first(c):
        for i in remote_slots(c):
            send_copy(c, i).wait_recv()
        for i in range(3):
            gather_copy(c, i).start()

    def landed(c, i):
        dst = (
            agb.at[c, at(0, 1)],
            agb.at[c, at(3, 0)],
            agb.at[c, at(1, 0)],
            agb.at[c, at(3, 1)],
            agb.at[c, at(1, 1)],
            agb.at[c, at(2, 0), 0],
            agb.at[c, at(2, 0), 1],
            agb.at[c, at(2, 1)],
        )[i]
        remote(dst, dst, ag_ss.at[c, i], ag_rs.at[c, i], across).wait_recv()

    def gather_second(c):
        landed(c, 0)
        gather_copy(c, 3).start()
        gather_copy(c, 4).start()
        landed(c, 1)
        gather_copy(c, 5).start()
        landed(c, 2)
        gather_copy(c, 6).start()

    def gather_third(c):
        landed(c, 5)
        landed(c, 6)
        gather_copy(c, 7).start()

    def gather_last(c):
        for i in (3, 4, 7):
            landed(c, i)

    two = Reduce(parts2, y2a, p2, h2, t2, y2b, rs2_ss, rs2_rs)

    def experts(c):
        square = jnp.zeros((256, 1), jnp.float32)
        for f in range(8):
            piece = f32(agb[c, f].reshape(256, 256))
            square = square + jnp.sum(piece * piece, axis=1, keepdims=True)
        scale = lax.rsqrt(square * (1.0 / 2048) + EPSILON)
        for f in range(8):
            cols = slice(f * 256, (f + 1) * 256)
            piece = f32(agb[c, f].reshape(256, 256))
            normed[:, cols] = (piece * scale * gain_ref[:, cols]).astype(jnp.bfloat16)
        for e in range(2):
            rows = slice(e * 128, (e + 1) * 128)
            lifted = jnp.dot(normed[rows, :], up[e], preferred_element_type=jnp.float32)
            gated = jnp.dot(normed[rows, :], gate[e], preferred_element_type=jnp.float32)
            hidden = (gated / (1.0 + jnp.exp(-gated)) * lifted).astype(jnp.bfloat16)
            for f in range(8):
                parts2[c, f, rows, :] = jnp.dot(
                    hidden, down[e, :, f * 256 : (f + 1) * 256],
                    preferred_element_type=jnp.float32,
                ).astype(jnp.bfloat16)

    def finish(c):
        fin[c] = two.last(c).astype(jnp.bfloat16).reshape(2, 8, 16, 256)
        for i in remote_slots(c):
            back_copy(c, i).start()
        if c == 0:
            back[ctx] = fin[0, :, 0]

    for step in range(CHUNKS):
        gather_first(step)
        if step >= 1:
            gather_second(step - 1)
        if step >= 2:
            gather_third(step - 2)
    for load in loads:
        load.wait()
    for step in range(CHUNKS + 3):
        if step == 0:
            gather_second(3)
            gather_third(2)
        if step == 1:
            gather_third(3)
        if step < CHUNKS:
            gather_last(step)
            experts(step)
            two.first(step)
        if 0 <= step - 1 < CHUNKS:
            two.second(step - 1)
        if 0 <= step - 2 < CHUNKS:
            two.third(step - 2)
        if 0 <= step - 3 < CHUNKS:
            finish(step - 3)

    for c in range(CHUNKS):
        for i in remote_slots(c):
            dst = back.at[ctx_at(*slots[c][i])]
            remote(dst, dst, f_ss.at[c, i], f_rs.at[c, i], across).wait_recv()
    for rows in (slice(0, 256), slice(256, 512)):
        moved = jnp.dot(
            unpack_ref[rows, :], back[...].reshape(1024, 256), preferred_element_type=jnp.float32
        )
        out_ref[rows, :] = (f32(stream[rows, :]) + moved).astype(jnp.bfloat16)

    for c in range(2):
        one.drain(c)
    for c in range(CHUNKS):
        two.drain(c)
        for i in range(8):
            gather_copy(c, i).wait_send()
        for i in remote_slots(c):
            send_copy(c, i).wait_send()
            back_copy(c, i).wait_send()


def experts_layer(attended, out_weight, residual, gain, pack, unpack, gate, up, down):
    rows, width = residual.shape
    dma = pltpu.SemaphoreType.DMA
    vmem, hbm = pl.BlockSpec(memory_space=pltpu.VMEM), pl.BlockSpec(memory_space=pl.ANY)
    bf16 = jnp.bfloat16

    def reduce_buffers(chunks, height):
        return [
            pltpu.VMEM((chunks, 8, height, 256), bf16),
            pltpu.VMEM((chunks, height, 256), bf16),
            pltpu.VMEM((chunks, 2, height, 256), bf16),
            pltpu.VMEM((chunks, 2, height // 2, 256), bf16),
            pltpu.VMEM((chunks, 2, height, 256), bf16),
            pltpu.VMEM((chunks, height, 256), bf16),
        ]

    return pl.pallas_call(
        expert_kernel,
        out_shape=jax.ShapeDtypeStruct((rows, width), bf16),
        in_specs=[vmem] * 6 + [hbm] * 3,
        out_specs=vmem,
        scratch_shapes=[
            pltpu.VMEM(gate.shape, bf16),
            pltpu.VMEM(up.shape, bf16),
            pltpu.VMEM(down.shape, bf16),
            pltpu.VMEM((512, 256), bf16),
            pltpu.VMEM((32, 2, 16, 256), bf16),
            pltpu.VMEM((CHUNKS, 8, 2, 8, 16, 256), bf16),
            pltpu.VMEM((256, 2048), bf16),
            pltpu.VMEM((32, 2, 16, 256), bf16),
            pltpu.VMEM((CHUNKS, 2, 8, 16, 256), bf16),
        ]
        + reduce_buffers(2, 256)
        + reduce_buffers(CHUNKS, 256)
        + [
            dma((3,)),
            dma((2, 8)),
            dma((2, 8)),
            dma((CHUNKS, 8)),
            dma((CHUNKS, 8)),
            dma((CHUNKS, 8)),
            dma((CHUNKS, 8)),
            dma((CHUNKS, 8)),
            dma((CHUNKS, 8)),
            dma((CHUNKS, 8)),
            dma((CHUNKS, 8)),
        ],
        compiler_params=pltpu.CompilerParams(
            collective_id=1, has_side_effects=True, vmem_limit_bytes=VMEM_BYTES
        ),
        cost_estimate=pl.CostEstimate(flops=5 * 10**9, bytes_accessed=10**7, transcendentals=10**6),
    )(attended, out_weight, residual, gain, pack, unpack, gate, up, down)


def per_device(
    residual,
    query_vectors,
    key_vectors,
    value_vectors,
    out_weight,
    norm_gain,
    species,
    gate_weight,
    up_weight,
    down_weight,
):
    expert_ids = species[:, 0]
    block_count = expert_ids.shape[0]
    order = jnp.arange(block_count)
    earlier = (expert_ids[None, :] == expert_ids[:, None]) & (order[None, :] < order[:, None])
    slot_ids = expert_ids * MOST + jnp.sum(earlier, axis=1, dtype=jnp.int32)
    row_ids = (slot_ids[:, None] * BLK + jnp.arange(BLK, dtype=jnp.int32)[None, :]).reshape(-1)
    places = jnp.arange(64 * MOST * BLK, dtype=jnp.int32)
    pack = (places[:, None] == row_ids[None, :]).astype(jnp.bfloat16)
    unpack = (row_ids[:, None] == places[None, :]).astype(jnp.bfloat16)
    attended = attention(query_vectors, key_vectors, value_vectors)
    return experts_layer(
        attended, out_weight, residual, norm_gain.reshape(1, -1), pack, unpack,
        gate_weight, up_weight, down_weight,
    )


def solution(mesh):
    return jax.shard_map(
        per_device,
        mesh=mesh,
        in_specs=(
            P("ctx", "exp"),
            P("ctx", "exp"),
            P("ctx", "exp"),
            P("ctx", "exp"),
            P("exp", None),
            P(),
            P("ctx", None),
            P("ctx", None, "exp"),
            P("ctx", None, "exp"),
            P("ctx", "exp", None),
        ),
        out_specs=P("ctx", "exp"),
        check_vma=False,
    )
```

```python
import functools
import math

import jax
import jax.numpy as jnp
from jax import lax
from jax.experimental import pallas as pl
from jax.experimental.pallas import tpu as pltpu
from jax.sharding import PartitionSpec as P

HEAD_DIM = 128
BLK = 8
MOST = 2
EPSILON = 1e-06
EXP2_FACTOR = math.log2(math.e) / math.sqrt(HEAD_DIM)
VMEM_BYTES = 60 * 1024 * 1024
TILE_Q = 512
Z_CHUNKS = ((0, 1), (7, 2), (6, 3), (5, 4))
CHUNKS = len(Z_CHUNKS)
MESH = pl.DeviceIdType.MESH


def remote(src, dst, send_sem, recv_sem, where):
    return pltpu.make_async_remote_copy(
        src_ref=src,
        dst_ref=dst,
        send_sem=send_sem,
        recv_sem=recv_sem,
        device_id=where,
        device_id_type=MESH,
    )


def greet(others):
    barrier = pltpu.get_barrier_semaphore()
    for where in others:
        pl.semaphore_signal(barrier, inc=1, device_id=where, device_id_type=MESH)


def f32(value):
    return value.astype(jnp.float32)


def fused_kernel(
    q_ref, k_ref, v_ref, wo_ref, res_ref, gain_ref, ids_ref, gate_hbm, up_hbm, down_hbm,
    out_ref,
    qbuf, q_give, kv, kv_give, acc, top, o_send, att, wo_cols,
    gate, up, down, pack, unpack, stream, packed, agb, normed, back, fin,
    parts, ya, pp, hh, tt, yb,
    r_ss, r_rs, l_ss, l_rs, s_ss, s_rs, x_ss, x_rs, wo_ss, wo_rs, w_sem, a1_ss, a1_rs,
    rd_ss, rd_rs, ag_ss, ag_rs, b_ss, b_rs, f_ss, f_rs,
):
    ctx = lax.axis_index("ctx")
    z, lane = ctx // 4, ctx % 4
    exp = lax.axis_index("exp")
    x, y = exp % 4, exp // 4
    bf16 = jnp.bfloat16

    def at(dx, dy):
        return ((y + dy) % 2) * 4 + (x + dx) % 4

    def ctx_at(dz, dl):
        return ((z + dz) % 8) * 4 + (lane + dl) % 4

    me = at(0, 0)
    ahead, behind, across = {"exp": at(1, 0)}, {"exp": at(3, 0)}, {"exp": at(0, 1)}
    right, left = {"ctx": ctx_at(1, 0)}, {"ctx": ctx_at(7, 0)}
    sibling = {"ctx": z * 4 + (lane // 2) * 2 + (lane + 1) % 2}
    partner = {"ctx": ctx_at(0, 2)}

    exp_peers = [(dx, dy) for dy in range(2) for dx in range(4) if dx or dy]
    peers = [{"ctx": ctx_at(dz, dl)} for dz in range(8) for dl in range(4) if dz or dl]
    peers += [{"exp": at(dx, dy)} for dx, dy in exp_peers]
    greet(peers)
    loads = [
        pltpu.make_async_copy(src, dst, w_sem.at[i])
        for i, (src, dst) in enumerate(((gate_hbm, gate), (up_hbm, up), (down_hbm, down)))
    ]
    for load in loads:
        load.start()

    head, far_head = lane // 2, 1 - lane // 2
    mine = pl.ds(pl.multiple_of(head * HEAD_DIM, HEAD_DIM), HEAD_DIM)
    theirs = pl.ds(pl.multiple_of(far_head * HEAD_DIM, HEAD_DIM), HEAD_DIM)
    for place, cols in ((kv.at[0, 0, 0], mine), (kv_give, theirs)):
        for j in range(4):
            rows = slice(j * 128, (j + 1) * 128)
            place[0, j] = k_ref[rows, cols].T
            place[1, j] = v_ref[rows, cols]
    qbuf[0:512] = q_ref[:, mine]
    q_give[...] = q_ref[:, theirs]

    pl.semaphore_wait(pltpu.get_barrier_semaphore(), len(peers))

    def right_item(t):
        return 1 + t // 2, t % 2

    def left_item(t):
        return 7 - t // 2, t % 2 + t // 6

    def right_copy(t, p):
        slot, part = right_item(t)
        return remote(
            kv.at[0, slot - 1, part, p], kv.at[0, slot, part, p], r_ss.at[t, p], r_rs.at[t, p], right
        )

    def left_copy(t, p):
        slot, part = left_item(t)
        return remote(
            kv.at[0, (slot + 1) % 8, part, p],
            kv.at[0, slot, part, p],
            l_ss.at[t, p],
            l_rs.at[t, p],
            left,
        )

    def sibling_copy(way, t):
        slot, part = (right_item, left_item)[way](t)
        return remote(
            kv.at[0, slot, part], kv.at[1, slot, part], s_ss.at[way, t], s_rs.at[way, t], sibling
        )

    kv_copies = [
        remote(kv_give.at[p], kv.at[0, 0, 1, p], x_ss.at[p], x_rs.at[p], partner) for p in range(2)
    ]
    query_copy = remote(q_give, qbuf.at[pl.ds(512, 512)], x_ss.at[2], x_rs.at[2], partner)
    out_copy = remote(o_send, att.at[1, me], x_ss.at[3], x_rs.at[3], partner)
    near_copy = remote(kv.at[0, 0, 0], kv.at[1, 0, 0], x_ss.at[4], x_rs.at[4], sibling)
    far_copy = remote(kv.at[0, 0, 1], kv.at[1, 0, 1], x_ss.at[5], x_rs.at[5], sibling)
    for p in range(2):
        right_copy(0, p).start()
        left_copy(0, p).start()
        kv_copies[p].start()
    near_copy.start()
    query_copy.start()

    def wo_block(index):
        return pl.ds(pl.multiple_of(index * 256, 256), 256)

    def wo_copy(i):
        dx, dy = exp_peers[i]
        to = at(dx, dy)
        return remote(
            wo_ref.at[:, wo_block(to)], wo_cols.at[me], wo_ss.at[i], wo_rs.at[i], {"exp": to}
        )

    acc[...] = jnp.zeros_like(acc)
    top[...] = jnp.full_like(top, -1e30)
    ones = jnp.ones((512, HEAD_DIM), bf16)

    def attend(first, count, chunks):
        def one_tile(index, unused):
            rows = pl.ds(pl.multiple_of(first + index * TILE_Q, TILE_Q), TILE_Q)
            q = qbuf[rows, :]
            scores = [
                jnp.dot(
                    q,
                    jnp.concatenate([kv[kind, slot, part, 0, j] for j in range(4)], axis=1),
                    preferred_element_type=jnp.float32,
                )
                for kind, slot, part in chunks
            ]
            before = top[rows, :]
            best = functools.reduce(jnp.maximum, scores)
            best = jnp.maximum(best[:, :256], best[:, 256:])
            best = jnp.maximum(best[:, :128], best[:, 128:])
            now = jnp.maximum(before, jnp.max(best, axis=1, keepdims=True))
            top[rows, :] = now
            wide_now = jnp.concatenate([now] * 4, axis=1)
            total = None
            for s, (kind, slot, part) in zip(scores, chunks):
                weights = jnp.exp2((s - wide_now) * EXP2_FACTOR).astype(bf16)
                wide = jnp.concatenate([kv[kind, slot, part, 1].reshape(512, 128), ones], axis=1)
                term = jnp.dot(weights, wide, preferred_element_type=jnp.float32)
                total = term if total is None else total + term
            shrink = jnp.exp2((before - now) * EXP2_FACTOR)
            acc[rows, :] = acc[rows, :] * jnp.concatenate([shrink, shrink], axis=1) + total
            return unused

        lax.fori_loop(0, count // TILE_Q, one_tile, 0)

    attend(0, 512, [(0, 0, 0)])
    near_copy.wait_recv()
    attend(0, 512, [(1, 0, 0)])
    def counter(shape, dim):
        return lax.broadcasted_iota(jnp.int32, shape, dim)

    def flag(condition):
        return jnp.where(condition, 1.0, 0.0)

    ids = jnp.broadcast_to(f32(ids_ref[...]), (64, 64))
    ids_t = ids.T
    same = flag(ids == ids_t)
    before_row = flag(counter((64, 64), 0) < counter((64, 64), 1))
    before_col = flag(counter((64, 64), 1) < counter((64, 64), 0))
    slot_row = MOST * ids[0:1, :] + jnp.sum(same * before_row, axis=0, keepdims=True)
    slot_col = MOST * ids_t[:, 0:1] + jnp.sum(same * before_col, axis=1, keepdims=True)
    spans = flag(counter((64, 512), 1) // BLK == counter((64, 512), 0)).astype(bf16)
    spans_t = flag(counter((512, 64), 0) // BLK == counter((512, 64), 1)).astype(bf16)
    token_row = jnp.dot(
        jnp.broadcast_to(slot_row, (8, 64)).astype(bf16), spans, preferred_element_type=jnp.float32
    ).astype(jnp.int32)[0:1, :] * BLK + counter((1, 512), 1) % BLK
    token_col = jnp.dot(
        spans_t, jnp.broadcast_to(slot_col, (64, 128)).astype(bf16),
        preferred_element_type=jnp.float32,
    ).astype(jnp.int32) * BLK + counter((512, 128), 0) % BLK
    for part in range(4):
        places = counter((256, 512), 0) + part * 256
        pack[part * 256 : (part + 1) * 256, :] = flag(places == token_row).astype(bf16)
    for part in range(8):
        places = counter((512, 128), 1) + part * 128
        unpack[:, part * 128 : (part + 1) * 128] = flag(places == token_col).astype(bf16)
    for p in range(2):
        kv_copies[p].wait_recv()
        right_copy(1, p).start()
        left_copy(1, p).start()
    far_copy.start()
    attend(0, 512, [(0, 0, 1)])
    for i in range(7):
        wo_copy(i).start()
    wo_cols[me] = wo_ref[:, wo_block(me)]

    def pass_on(t):
        for p in range(2):
            right_copy(t, p).wait_recv()

            @pl.when(t < 5)
            def _():
                right_copy(t + 2, p).start()

            left_copy(t, p).wait_recv()

            @pl.when(t < 4)
            def _():
                left_copy(t + 2, p).start()

            @pl.when(t == 5)
            def _():
                left_copy(6, p).start()

        sibling_copy(0, t).start()
        sibling_copy(1, t).start()

    def stage(t, unused):
        pass_on(t)

        @pl.when(t == 0)
        def _():
            query_copy.wait_recv()
            far_copy.wait_recv()

        @pl.when(t < 5)
        def _():
            attend(512 * (1 - t // 4), 512, [(t % 2 + t // 4, 0, t // 2 - t // 4)])

        attend(0, 1024, [(0,) + right_item(t), (0,) + left_item(t)])
        sibling_copy(0, t).wait_recv()
        sibling_copy(1, t).wait_recv()
        attend(0, 1024, [(1,) + right_item(t), (1,) + left_item(t)])
        return unused

    lax.fori_loop(0, 6, stage, 0)

    def spread_copy(c, i):
        low, high = pl.ds(0, 256), pl.ds(256, 256)
        src, where = (
            (att.at[c, me], across),
            (att.at[c, me], ahead),
            (att.at[c, me], behind),
            (att.at[c, at(0, 1)], ahead),
            (att.at[c, at(0, 1)], behind),
            (att.at[c, at(3, 0), low], ahead),
            (att.at[c, at(1, 0), high], behind),
            (att.at[c, at(2, 0)], across),
        )[i]
        return remote(src, src, a1_ss.at[c, i], a1_rs.at[c, i], where)

    def spread_landed(c, i):
        low, high = pl.ds(0, 256), pl.ds(256, 256)
        dst = (
            att.at[c, at(0, 1)],
            att.at[c, at(3, 0)],
            att.at[c, at(1, 0)],
            att.at[c, at(3, 1)],
            att.at[c, at(1, 1)],
            att.at[c, at(2, 0), low],
            att.at[c, at(2, 0), high],
            att.at[c, at(2, 1)],
        )[i]
        remote(dst, dst, a1_ss.at[c, i], a1_rs.at[c, i], across).wait_recv()

    pass_on(6)
    attend(0, 512, [(0, 4, 0), (0, 4, 1)])
    sibling_copy(0, 6).wait_recv()
    sibling_copy(1, 6).wait_recv()
    attend(0, 512, [(1, 4, 0), (1, 4, 1)])
    att[0, me] = (acc[:512, :HEAD_DIM] / acc[:512, HEAD_DIM:]).astype(bf16)
    for i in range(3):
        spread_copy(0, i).start()
    attend(512, 512, [(0, 4, 0), (0, 4, 1)])
    attend(512, 512, [(1, 4, 0), (1, 4, 1)])
    o_send[...] = (acc[512:, :HEAD_DIM] / acc[512:, HEAD_DIM:]).astype(bf16)
    out_copy.start()
    for c in range(2):
        if c == 1:
            out_copy.wait_recv()
            for i in range(3):
                spread_copy(1, i).start()
        for i, nexts in ((0, (3, 4)), (1, (5,)), (2, (6,))):
            spread_landed(c, i)
            for n in nexts:
                spread_copy(c, n).start()
    for c in range(2):
        spread_landed(c, 5)
        spread_landed(c, 6)
        spread_copy(c, 7).start()
    for i in range(7):
        dx, dy = exp_peers[i]
        dst = wo_cols.at[at(4 - dx, dy)]
        remote(dst, dst, wo_ss.at[i], wo_rs.at[i], across).wait_recv()
    for c in range(2):
        for i in (3, 4, 7):
            spread_landed(c, i)
    near_rows, far_rows = mine, theirs
    for part in range(2):
        rows = slice(part * 256, (part + 1) * 256)
        total = f32(res_ref[rows, :])
        for f in range(8):
            total = total + jnp.dot(
                jnp.concatenate([att[0, f, rows, :], att[1, f, rows, :]], axis=1),
                jnp.concatenate([wo_cols[f, near_rows, :], wo_cols[f, far_rows, :]], axis=0),
                preferred_element_type=jnp.float32,
            )
        stream[rows, :] = total.astype(bf16)

    slots = [
        [(dz, dl) for dz in pair for dl in range(4)] for pair in Z_CHUNKS
    ]

    def send_copy(c, i):
        dz, dl = slots[c][i]
        to = ctx_at(dz, dl)
        return remote(
            packed.at[to], agb.at[c, me, :, i], b_ss.at[c, i], b_rs.at[c, i], {"ctx": to}
        )

    def back_copy(c, i):
        dz, dl = slots[c][i]
        to = ctx_at(8 - dz, 4 - dl)
        return remote(
            fin.at[c, :, i], back.at[ctx], f_ss.at[c, i], f_rs.at[c, i], {"ctx": to}
        )

    def remote_slots(c):
        return [i for i in range(8) if slots[c][i] != (0, 0)]

    for part in range(4):
        packed[part * 8 : (part + 1) * 8] = jnp.dot(
            pack[part * 256 : (part + 1) * 256, :], stream[...],
            preferred_element_type=jnp.float32,
        ).astype(jnp.bfloat16).reshape(8, 2, 16, 256)
    for c in range(CHUNKS):
        for i in remote_slots(c):
            send_copy(c, i).start()
    agb[0, me, :, 0] = packed[ctx]

    def gather_copy(c, i):
        src, where = (
            (agb.at[c, me], across),
            (agb.at[c, me], ahead),
            (agb.at[c, me], behind),
            (agb.at[c, at(0, 1)], ahead),
            (agb.at[c, at(0, 1)], behind),
            (agb.at[c, at(3, 0), 0], ahead),
            (agb.at[c, at(1, 0), 1], behind),
            (agb.at[c, at(2, 0)], across),
        )[i]
        return remote(src, src, ag_ss.at[c, i], ag_rs.at[c, i], where)

    def gather_first(c):
        for i in remote_slots(c):
            send_copy(c, i).wait_recv()
        for i in range(3):
            gather_copy(c, i).start()

    def landed(c, i):
        dst = (
            agb.at[c, at(0, 1)],
            agb.at[c, at(3, 0)],
            agb.at[c, at(1, 0)],
            agb.at[c, at(3, 1)],
            agb.at[c, at(1, 1)],
            agb.at[c, at(2, 0), 0],
            agb.at[c, at(2, 0), 1],
            agb.at[c, at(2, 1)],
        )[i]
        remote(dst, dst, ag_ss.at[c, i], ag_rs.at[c, i], across).wait_recv()

    def gather_second(c):
        landed(c, 0)
        gather_copy(c, 3).start()
        gather_copy(c, 4).start()
        landed(c, 1)
        gather_copy(c, 5).start()
        landed(c, 2)
        gather_copy(c, 6).start()

    def gather_third(c):
        landed(c, 5)
        landed(c, 6)
        gather_copy(c, 7).start()

    def gather_last(c):
        for i in (3, 4, 7):
            landed(c, i)

    half = 128
    low_rows, high_rows = pl.ds(0, half), pl.ds(half, half)

    def sum_copy(c, i):
        src, dst, where = (
            (parts.at[c, at(2, 1)], ya.at[c], across),
            (parts.at[c, at(1, 1)], pp.at[c, 0], ahead),
            (parts.at[c, at(3, 1)], pp.at[c, 1], behind),
            (parts.at[c, at(2, 0), low_rows], hh.at[c, 0], ahead),
            (parts.at[c, at(2, 0), high_rows], hh.at[c, 1], behind),
            (parts.at[c, at(1, 0)], tt.at[c, 0], ahead),
            (parts.at[c, at(3, 0)], tt.at[c, 1], behind),
            (parts.at[c, at(0, 1)], yb.at[c], across),
        )[i]
        return remote(src, dst, rd_ss.at[c, i], rd_rs.at[c, i], where)

    def sum_first(c):
        for i in range(3):
            sum_copy(c, i).start()

    def sum_second(c):
        sum_copy(c, 0).wait_recv()
        far = at(2, 0)
        parts[c, far] = (f32(parts[c, far]) + f32(ya[c])).astype(bf16)
        sum_copy(c, 3).start()
        sum_copy(c, 4).start()

    def sum_third(c):
        sum_copy(c, 1).wait_recv()
        sum_copy(c, 2).wait_recv()
        other = at(0, 1)
        parts[c, other] = (f32(parts[c, other]) + f32(pp[c, 0]) + f32(pp[c, 1])).astype(bf16)
        sum_copy(c, 7).start()
        for way, rows in ((0, low_rows), (1, high_rows)):
            sum_copy(c, 3 + way).wait_recv()
            near = at(1 if way == 0 else 3, 0)
            parts[c, near, rows] = (f32(parts[c, near, rows]) + f32(hh[c, way])).astype(bf16)
            sum_copy(c, 5 + way).start()

    def sum_last(c):
        for i in (5, 6, 7):
            sum_copy(c, i).wait_recv()
        return (f32(parts[c, me]) + f32(tt[c, 0])) + (f32(tt[c, 1]) + f32(yb[c]))

    def experts(c):
        square = jnp.zeros((256, 1), jnp.float32)
        for f in range(8):
            piece = f32(agb[c, f].reshape(256, 256))
            square = square + jnp.sum(piece * piece, axis=1, keepdims=True)
        scale = lax.rsqrt(square * (1.0 / 2048) + EPSILON)
        for f in range(8):
            cols = slice(f * 256, (f + 1) * 256)
            piece = f32(agb[c, f].reshape(256, 256))
            normed[:, cols] = (piece * scale * gain_ref[:, cols]).astype(jnp.bfloat16)
        for e in range(2):
            rows = slice(e * 128, (e + 1) * 128)
            lifted = lax.dot_general(
                normed[rows, :], up[e], (((1,), (1,)), ((), ())),
                preferred_element_type=jnp.float32,
            )
            gated = lax.dot_general(
                normed[rows, :], gate[e], (((1,), (1,)), ((), ())),
                preferred_element_type=jnp.float32,
            )
            hidden = (gated / (1.0 + jnp.exp(-gated)) * lifted).astype(jnp.bfloat16)
            for f in range(8):
                parts[c, f, rows, :] = jnp.dot(
                    hidden, down[e, :, f * 256 : (f + 1) * 256],
                    preferred_element_type=jnp.float32,
                ).astype(jnp.bfloat16)

    def finish(c):
        fin[c] = sum_last(c).astype(jnp.bfloat16).reshape(2, 8, 16, 256)
        for i in remote_slots(c):
            back_copy(c, i).start()
        if c == 0:
            back[ctx] = fin[0, :, 0]

    for step in range(CHUNKS):
        gather_first(step)
        if step >= 1:
            gather_second(step - 1)
        if step >= 2:
            gather_third(step - 2)
    for load in loads:
        load.wait()
    for step in range(CHUNKS + 3):
        if step == 0:
            gather_second(3)
            gather_third(2)
        if step == 1:
            gather_third(3)
        if step < CHUNKS:
            gather_last(step)
            experts(step)
            sum_first(step)
        if 0 <= step - 1 < CHUNKS:
            sum_second(step - 1)
        if 0 <= step - 2 < CHUNKS:
            sum_third(step - 2)
        if 0 <= step - 3 < CHUNKS:
            finish(step - 3)

    for c in range(CHUNKS):
        for i in remote_slots(c):
            dst = back.at[ctx_at(*slots[c][i])]
            remote(dst, dst, f_ss.at[c, i], f_rs.at[c, i], across).wait_recv()
    for rows in (slice(0, 256), slice(256, 512)):
        moved = jnp.dot(
            unpack[rows, :], back[...].reshape(1024, 256), preferred_element_type=jnp.float32
        )
        out_ref[rows, :] = (f32(stream[rows, :]) + moved).astype(jnp.bfloat16)

    def drain(t, unused):
        for p in range(2):
            right_copy(t, p).wait_send()
            left_copy(t, p).wait_send()
        sibling_copy(0, t).wait_send()
        sibling_copy(1, t).wait_send()
        return unused

    lax.fori_loop(0, 7, drain, 0)
    for copy in kv_copies + [query_copy, out_copy, near_copy, far_copy]:
        copy.wait_send()
    for i in range(7):
        wo_copy(i).wait_send()
    for c in range(2):
        for i in range(8):
            spread_copy(c, i).wait_send()
    for c in range(CHUNKS):
        for i in range(8):
            sum_copy(c, i).wait_send()
            gather_copy(c, i).wait_send()
        for i in remote_slots(c):
            send_copy(c, i).wait_send()
            back_copy(c, i).wait_send()


def layer(q, k, v, out_weight, residual, gain, ids, gate, up, down):
    rows, width = residual.shape
    dma = pltpu.SemaphoreType.DMA
    vmem, hbm = pl.BlockSpec(memory_space=pltpu.VMEM), pl.BlockSpec(memory_space=pl.ANY)
    bf16, single = jnp.bfloat16, jnp.float32
    pairs = [(7, 2), (7, 2), (2, 7), (6,), (7,)]
    sems = [dma(shape) for shape in pairs for _ in range(2)]
    return pl.pallas_call(
        fused_kernel,
        out_shape=jax.ShapeDtypeStruct((rows, width), bf16),
        in_specs=[vmem] * 7 + [hbm] * 3,
        out_specs=vmem,
        scratch_shapes=[
            pltpu.VMEM((1024, HEAD_DIM), bf16),
            pltpu.VMEM((512, HEAD_DIM), bf16),
            pltpu.VMEM((2, 8, 2, 2, 4, 128, 128), bf16),
            pltpu.VMEM((2, 4, 128, 128), bf16),
            pltpu.VMEM((1024, 2 * HEAD_DIM), single),
            pltpu.VMEM((1024, HEAD_DIM), single),
            pltpu.VMEM((512, HEAD_DIM), bf16),
            pltpu.VMEM((2, 8, 512, HEAD_DIM), bf16),
            pltpu.VMEM((8, 256, 256), bf16),
            pltpu.VMEM(gate.shape, bf16),
            pltpu.VMEM(up.shape, bf16),
            pltpu.VMEM(down.shape, bf16),
            pltpu.VMEM((1024, 512), bf16),
            pltpu.VMEM((512, 1024), bf16),
            pltpu.VMEM((512, 256), bf16),
            pltpu.VMEM((32, 2, 16, 256), bf16),
            pltpu.VMEM((CHUNKS, 8, 2, 8, 16, 256), bf16),
            pltpu.VMEM((256, 2048), bf16),
            pltpu.VMEM((32, 2, 16, 256), bf16),
            pltpu.VMEM((CHUNKS, 2, 8, 16, 256), bf16),
            pltpu.VMEM((CHUNKS, 8, 256, 256), bf16),
            pltpu.VMEM((CHUNKS, 256, 256), bf16),
            pltpu.VMEM((CHUNKS, 2, 256, 256), bf16),
            pltpu.VMEM((CHUNKS, 2, 128, 256), bf16),
            pltpu.VMEM((CHUNKS, 2, 256, 256), bf16),
            pltpu.VMEM((CHUNKS, 256, 256), bf16),
        ]
        + sems
        + [dma((3,)), dma((2, 8)), dma((2, 8))]
        + [dma((CHUNKS, 8)) for _ in range(8)],
        compiler_params=pltpu.CompilerParams(
            collective_id=0, has_side_effects=True, vmem_limit_bytes=VMEM_BYTES
        ),
        cost_estimate=pl.CostEstimate(
            flops=15 * 10**9, bytes_accessed=10**7, transcendentals=512 * 16384 * 2
        ),
    )(q, k, v, out_weight, residual, gain, ids, gate, up, down)


def per_device(
    residual,
    query_vectors,
    key_vectors,
    value_vectors,
    out_weight,
    norm_gain,
    species,
    gate_weight,
    up_weight,
    down_weight,
):
    return layer(
        query_vectors, key_vectors, value_vectors, out_weight, residual, norm_gain.reshape(1, -1),
        species.reshape(1, -1), jnp.swapaxes(gate_weight, 1, 2), jnp.swapaxes(up_weight, 1, 2), down_weight,
    )


def solution(mesh):
    return jax.shard_map(
        per_device,
        mesh=mesh,
        in_specs=(
            P("ctx", "exp"),
            P("ctx", "exp"),
            P("ctx", "exp"),
            P("ctx", "exp"),
            P("exp", None),
            P(),
            P("ctx", None),
            P("ctx", None, "exp"),
            P("ctx", None, "exp"),
            P("ctx", "exp", None),
        ),
        out_specs=P("ctx", "exp"),
        check_vma=False,
    )
```

```python
import functools
import math

import jax
import jax.numpy as jnp
from jax import lax
from jax.experimental import pallas as pl
from jax.experimental.pallas import tpu as pltpu
from jax.sharding import PartitionSpec as P

HEAD_DIM = 128
BLK = 8
MOST = 2
EPSILON = 1e-06
EXP2_FACTOR = math.log2(math.e) / math.sqrt(HEAD_DIM)
VMEM_BYTES = 60 * 1024 * 1024
TILE_Q = 512
Z_ORDER = (0, 1, 7, 2, 6, 3, 5, 4)
CHUNKS = ((0, 1), (1, 2), (2, 4), (4, 6), (6, 7), (7, 8))
ORDER = (
    (0, 0), (0, 1), (1, 0), (1, 1), (0, 2), (2, 0), (0, 3), (2, 1), (3, 0), (1, 2),
    (4, 0), (0, 4), (0, 5), (1, 3), (3, 1), (5, 0), (4, 1), (2, 2), (5, 1), (1, 4),
    (6, 0), (1, 5), (3, 2), (2, 3), (4, 2), (5, 2), (2, 4), (6, 1), (7, 0), (8, 0),
    (3, 3), (4, 3), (5, 3), (2, 5), (7, 1), (6, 2), (3, 4), (8, 1), (4, 4), (5, 4),
    (7, 2), (6, 3), (8, 2), (3, 5), (4, 5), (5, 5), (7, 3), (6, 4), (8, 3), (9, 0),
    (9, 1), (7, 4), (6, 5), (7, 5), (9, 2), (8, 4), (9, 3), (8, 5), (9, 4), (9, 5),
)
MESH = pl.DeviceIdType.MESH


def remote(src, dst, send_sem, recv_sem, where):
    return pltpu.make_async_remote_copy(
        src_ref=src,
        dst_ref=dst,
        send_sem=send_sem,
        recv_sem=recv_sem,
        device_id=where,
        device_id_type=MESH,
    )


def greet(others):
    barrier = pltpu.get_barrier_semaphore()
    for where in others:
        pl.semaphore_signal(barrier, inc=1, device_id=where, device_id_type=MESH)


def f32(value):
    return value.astype(jnp.float32)


def fused_kernel(
    q_ref, k_ref, v_ref, wo_ref, res_ref, gain_ref, ids_ref, gate_hbm, up_hbm, down_hbm,
    out_ref,
    qbuf, q_give, kv, kv_give, acc, top, o_send, att, wo_cols,
    gate, up, down, pack, unpack, stream, packed, agb, normed, back, fin,
    parts, ya, pp, hh, tt, yb, yc,
    r_ss, r_rs, l_ss, l_rs, s_ss, s_rs, x_ss, x_rs, wo_ss, wo_rs, w_sem, a1_ss, a1_rs,
    rd_ss, rd_rs, ag_ss, ag_rs, b_ss, b_rs, f_ss, f_rs,
):
    ctx = lax.axis_index("ctx")
    z, lane = ctx // 4, ctx % 4
    exp = lax.axis_index("exp")
    x, y = exp % 4, exp // 4
    bf16 = jnp.bfloat16

    def at(dx, dy):
        return ((y + dy) % 2) * 4 + (x + dx) % 4

    def ctx_at(dz, dl):
        return ((z + dz) % 8) * 4 + (lane + dl) % 4

    me = at(0, 0)
    ahead, behind, across = {"exp": at(1, 0)}, {"exp": at(3, 0)}, {"exp": at(0, 1)}
    right, left = {"ctx": ctx_at(1, 0)}, {"ctx": ctx_at(7, 0)}
    sibling = {"ctx": z * 4 + (lane // 2) * 2 + (lane + 1) % 2}
    partner = {"ctx": ctx_at(0, 2)}

    exp_peers = [(dx, dy) for dy in range(2) for dx in range(4) if dx or dy]
    peers = [{"ctx": ctx_at(dz, dl)} for dz in range(8) for dl in range(4) if dz or dl]
    peers += [{"exp": at(dx, dy)} for dx, dy in exp_peers]
    greet(peers)
    loads = [
        pltpu.make_async_copy(src, dst, w_sem.at[i])
        for i, (src, dst) in enumerate(((gate_hbm, gate), (up_hbm, up), (down_hbm, down)))
    ]
    for load in loads:
        load.start()

    head, far_head = lane // 2, 1 - lane // 2
    mine = pl.ds(pl.multiple_of(head * HEAD_DIM, HEAD_DIM), HEAD_DIM)
    theirs = pl.ds(pl.multiple_of(far_head * HEAD_DIM, HEAD_DIM), HEAD_DIM)
    for place, cols in ((kv.at[0, 0, 0], mine), (kv_give, theirs)):
        for j in range(4):
            rows = slice(j * 128, (j + 1) * 128)
            place[0, j] = k_ref[rows, cols].T
            place[1, j] = v_ref[rows, cols]
    qbuf[0:512] = q_ref[:, mine]
    q_give[...] = q_ref[:, theirs]

    pl.semaphore_wait(pltpu.get_barrier_semaphore(), len(peers))

    def right_item(t):
        return 1 + t // 2, t % 2

    def left_item(t):
        return 7 - t // 2, t % 2 + t // 6

    def right_copy(t, p):
        slot, part = right_item(t)
        return remote(
            kv.at[0, slot - 1, part, p], kv.at[0, slot, part, p], r_ss.at[t, p], r_rs.at[t, p], right
        )

    def left_copy(t, p):
        slot, part = left_item(t)
        return remote(
            kv.at[0, (slot + 1) % 8, part, p],
            kv.at[0, slot, part, p],
            l_ss.at[t, p],
            l_rs.at[t, p],
            left,
        )

    def sibling_copy(way, t):
        slot, part = (right_item, left_item)[way](t)
        return remote(
            kv.at[0, slot, part], kv.at[1, slot, part], s_ss.at[way, t], s_rs.at[way, t], sibling
        )

    kv_copies = [
        remote(kv_give.at[p], kv.at[0, 0, 1, p], x_ss.at[p], x_rs.at[p], partner) for p in range(2)
    ]
    query_copy = remote(q_give, qbuf.at[pl.ds(512, 512)], x_ss.at[2], x_rs.at[2], partner)
    out_copy = remote(o_send, att.at[1, me], x_ss.at[3], x_rs.at[3], partner)
    near_copy = remote(kv.at[0, 0, 0], kv.at[1, 0, 0], x_ss.at[4], x_rs.at[4], sibling)
    far_copy = remote(kv.at[0, 0, 1], kv.at[1, 0, 1], x_ss.at[5], x_rs.at[5], sibling)
    for p in range(2):
        right_copy(0, p).start()
        left_copy(0, p).start()
        kv_copies[p].start()
    near_copy.start()
    query_copy.start()

    def wo_block(index):
        return pl.ds(pl.multiple_of(index * 256, 256), 256)

    def wo_copy(i):
        dx, dy = exp_peers[i]
        to = at(dx, dy)
        return remote(
            wo_ref.at[:, wo_block(to)], wo_cols.at[me], wo_ss.at[i], wo_rs.at[i], {"exp": to}
        )

    acc[...] = jnp.zeros_like(acc)
    top[...] = jnp.full_like(top, -1e30)
    ones = jnp.ones((512, HEAD_DIM), bf16)

    def attend(first, count, chunks):
        def one_tile(index, unused):
            rows = pl.ds(pl.multiple_of(first + index * TILE_Q, TILE_Q), TILE_Q)
            q = qbuf[rows, :]
            scores = [
                jnp.dot(
                    q,
                    jnp.concatenate([kv[kind, slot, part, 0, j] for j in range(4)], axis=1),
                    preferred_element_type=jnp.float32,
                )
                for kind, slot, part in chunks
            ]
            before = top[rows, :]
            best = functools.reduce(jnp.maximum, scores)
            best = jnp.maximum(best[:, :256], best[:, 256:])
            best = jnp.maximum(best[:, :128], best[:, 128:])
            now = jnp.maximum(before, jnp.max(best, axis=1, keepdims=True))
            top[rows, :] = now
            wide_now = jnp.concatenate([now] * 4, axis=1)
            total = None
            for s, (kind, slot, part) in zip(scores, chunks):
                weights = jnp.exp2((s - wide_now) * EXP2_FACTOR).astype(bf16)
                wide = jnp.concatenate([kv[kind, slot, part, 1].reshape(512, 128), ones], axis=1)
                term = jnp.dot(weights, wide, preferred_element_type=jnp.float32)
                total = term if total is None else total + term
            shrink = jnp.exp2((before - now) * EXP2_FACTOR)
            acc[rows, :] = acc[rows, :] * jnp.concatenate([shrink, shrink], axis=1) + total
            return unused

        lax.fori_loop(0, count // TILE_Q, one_tile, 0)

    attend(0, 512, [(0, 0, 0)])
    near_copy.wait_recv()
    attend(0, 512, [(1, 0, 0)])
    def counter(shape, dim):
        return lax.broadcasted_iota(jnp.int32, shape, dim)

    def flag(condition):
        return jnp.where(condition, 1.0, 0.0)

    ids = jnp.broadcast_to(f32(ids_ref[...]), (64, 64))
    ids_t = ids.T
    same = flag(ids == ids_t)
    before_row = flag(counter((64, 64), 0) < counter((64, 64), 1))
    before_col = flag(counter((64, 64), 1) < counter((64, 64), 0))
    slot_row = MOST * ids[0:1, :] + jnp.sum(same * before_row, axis=0, keepdims=True)
    slot_col = MOST * ids_t[:, 0:1] + jnp.sum(same * before_col, axis=1, keepdims=True)
    spans = flag(counter((64, 512), 1) // BLK == counter((64, 512), 0)).astype(bf16)
    spans_t = flag(counter((512, 64), 0) // BLK == counter((512, 64), 1)).astype(bf16)
    token_row = jnp.dot(
        jnp.broadcast_to(slot_row, (8, 64)).astype(bf16), spans, preferred_element_type=jnp.float32
    ).astype(jnp.int32)[0:1, :] * BLK + counter((1, 512), 1) % BLK
    token_col = jnp.dot(
        spans_t, jnp.broadcast_to(slot_col, (64, 128)).astype(bf16),
        preferred_element_type=jnp.float32,
    ).astype(jnp.int32) * BLK + counter((512, 128), 0) % BLK
    for part in range(4):
        places = counter((256, 512), 0) + part * 256
        pack[part * 256 : (part + 1) * 256, :] = flag(places == token_row).astype(bf16)
    for part in range(8):
        places = counter((512, 128), 1) + part * 128
        unpack[:, part * 128 : (part + 1) * 128] = flag(places == token_col).astype(bf16)
    for p in range(2):
        kv_copies[p].wait_recv()
        right_copy(1, p).start()
        left_copy(1, p).start()
    far_copy.start()
    attend(0, 512, [(0, 0, 1)])
    for i in range(7):
        wo_copy(i).start()
    wo_cols[me] = wo_ref[:, wo_block(me)]

    def pass_on(t):
        for p in range(2):
            right_copy(t, p).wait_recv()

            @pl.when(t < 5)
            def _():
                right_copy(t + 2, p).start()

            left_copy(t, p).wait_recv()

            @pl.when(t < 4)
            def _():
                left_copy(t + 2, p).start()

            @pl.when(t == 5)
            def _():
                left_copy(6, p).start()

        sibling_copy(0, t).start()
        sibling_copy(1, t).start()

    def stage(t, unused):
        pass_on(t)

        @pl.when(t == 0)
        def _():
            query_copy.wait_recv()
            far_copy.wait_recv()

        @pl.when(t < 5)
        def _():
            attend(512 * (1 - t // 4), 512, [(t % 2 + t // 4, 0, t // 2 - t // 4)])

        attend(0, 1024, [(0,) + right_item(t), (0,) + left_item(t)])
        sibling_copy(0, t).wait_recv()
        sibling_copy(1, t).wait_recv()
        attend(0, 1024, [(1,) + right_item(t), (1,) + left_item(t)])
        return unused

    lax.fori_loop(0, 6, stage, 0)

    def spread_copy(c, i):
        low, high = pl.ds(0, 256), pl.ds(256, 256)
        src, where = (
            (att.at[c, me], across),
            (att.at[c, me], ahead),
            (att.at[c, me], behind),
            (att.at[c, at(0, 1)], ahead),
            (att.at[c, at(0, 1)], behind),
            (att.at[c, at(3, 0), low], ahead),
            (att.at[c, at(1, 0), high], behind),
            (att.at[c, at(2, 0)], across),
        )[i]
        return remote(src, src, a1_ss.at[c, i], a1_rs.at[c, i], where)

    def spread_landed(c, i):
        low, high = pl.ds(0, 256), pl.ds(256, 256)
        dst = (
            att.at[c, at(0, 1)],
            att.at[c, at(3, 0)],
            att.at[c, at(1, 0)],
            att.at[c, at(3, 1)],
            att.at[c, at(1, 1)],
            att.at[c, at(2, 0), low],
            att.at[c, at(2, 0), high],
            att.at[c, at(2, 1)],
        )[i]
        remote(dst, dst, a1_ss.at[c, i], a1_rs.at[c, i], across).wait_recv()

    pass_on(6)
    attend(0, 512, [(0, 4, 0), (0, 4, 1)])
    sibling_copy(0, 6).wait_recv()
    sibling_copy(1, 6).wait_recv()
    attend(0, 512, [(1, 4, 0), (1, 4, 1)])
    att[0, me] = (acc[:512, :HEAD_DIM] / acc[:512, HEAD_DIM:]).astype(bf16)
    for i in range(3):
        spread_copy(0, i).start()
    attend(512, 512, [(0, 4, 0), (0, 4, 1)])
    attend(512, 512, [(1, 4, 0), (1, 4, 1)])
    o_send[...] = (acc[512:, :HEAD_DIM] / acc[512:, HEAD_DIM:]).astype(bf16)
    out_copy.start()
    for c in range(2):
        if c == 1:
            out_copy.wait_recv()
            for i in range(3):
                spread_copy(1, i).start()
        for i, nexts in ((0, (3, 4)), (1, (5,)), (2, (6,))):
            spread_landed(c, i)
            for n in nexts:
                spread_copy(c, n).start()
    for c in range(2):
        spread_landed(c, 5)
        spread_landed(c, 6)
        spread_copy(c, 7).start()
    for i in range(7):
        dx, dy = exp_peers[i]
        dst = wo_cols.at[at(4 - dx, dy)]
        remote(dst, dst, wo_ss.at[i], wo_rs.at[i], across).wait_recv()
    for c in range(2):
        for i in (3, 4, 7):
            spread_landed(c, i)
    near_rows, far_rows = mine, theirs
    for part in range(2):
        rows = slice(part * 256, (part + 1) * 256)
        total = f32(res_ref[rows, :])
        for f in range(8):
            total = total + jnp.dot(
                jnp.concatenate([att[0, f, rows, :], att[1, f, rows, :]], axis=1),
                jnp.concatenate([wo_cols[f, near_rows, :], wo_cols[f, far_rows, :]], axis=0),
                preferred_element_type=jnp.float32,
            )
        stream[rows, :] = total.astype(bf16)

    slots = [(n, dl) for n in range(8) for dl in range(4)]

    def remote_slots(c):
        return [s for s in slots if s[0] in range(*CHUNKS[c]) and s != (0, 0)]

    def send_copy(n, dl):
        to = ctx_at(Z_ORDER[n], dl)
        return remote(
            packed.at[to], agb.at[me, n, :, dl], b_ss.at[n, dl], b_rs.at[n, dl], {"ctx": to}
        )

    def back_copy(n, dl):
        to = ctx_at(8 - Z_ORDER[n], 4 - dl)
        return remote(
            fin.at[n, :, dl], back.at[ctx], f_ss.at[n, dl], f_rs.at[n, dl], {"ctx": to}
        )

    for part in range(4):
        packed[part * 8 : (part + 1) * 8] = jnp.dot(
            pack[part * 256 : (part + 1) * 256, :], stream[...],
            preferred_element_type=jnp.float32,
        ).astype(bf16).reshape(8, 2, 16, 256)
    for c in range(len(CHUNKS)):
        for slot in remote_slots(c):
            send_copy(*slot).start()
    agb[me, 0, :, 0] = packed[ctx]

    def span(c):
        return pl.ds(CHUNKS[c][0], CHUNKS[c][1] - CHUNKS[c][0])

    def some(c, way):
        return pl.ds(1, 3) if c % 2 == way else pl.ds(0, 4)

    def some_rows(c, way):
        return pl.ds(16, 48) if c % 2 == way else pl.ds(0, 64)

    def gather_copy(c, i):
        rows = span(c)
        src, where = (
            (agb.at[me, rows], across),
            (agb.at[me, rows], ahead),
            (agb.at[me, rows], behind),
            (agb.at[at(0, 1), rows, :, some(c, 0)], ahead),
            (agb.at[at(0, 1), rows, :, some(c, 1)], behind),
            (agb.at[at(3, 0), rows, 0], ahead),
            (agb.at[at(1, 0), rows, 1], behind),
            (agb.at[at(2, 0), rows], across),
            (agb.at[at(3 if c % 2 == 0 else 1, 0), rows, :, pl.ds(0, 1)], across),
        )[i]
        return remote(src, src, ag_ss.at[c, i], ag_rs.at[c, i], where)

    def gather_first(c):
        for slot in remote_slots(c):
            send_copy(*slot).wait_recv()
        for i in range(3):
            gather_copy(c, i).start()

    def landed(c, i):
        rows = span(c)
        dst = (
            agb.at[at(0, 1), rows],
            agb.at[at(3, 0), rows],
            agb.at[at(1, 0), rows],
            agb.at[at(3, 1), rows, :, some(c, 0)],
            agb.at[at(1, 1), rows, :, some(c, 1)],
            agb.at[at(2, 0), rows, 0],
            agb.at[at(2, 0), rows, 1],
            agb.at[at(2, 1), rows],
            agb.at[at(3 if c % 2 == 0 else 1, 1), rows, :, pl.ds(0, 1)],
        )[i]
        remote(dst, dst, ag_ss.at[c, i], ag_rs.at[c, i], across).wait_recv()

    def gather_second(c):
        landed(c, 0)
        gather_copy(c, 3).start()
        gather_copy(c, 4).start()
        landed(c, 1)
        gather_copy(c, 5).start()
        landed(c, 2)
        gather_copy(c, 6).start()
        gather_copy(c, 8).start()

    def gather_third(c):
        landed(c, 5)
        landed(c, 6)
        gather_copy(c, 7).start()

    def gather_last(c):
        for i in (3, 4, 7, 8):
            landed(c, i)

    def sum_copy(c, i):
        rows = span(c)
        src, dst, where = (
            (parts.at[at(2, 1), rows], ya.at[rows], across),
            (parts.at[at(1, 1), rows, :, some_rows(c, 0)], pp.at[0, rows, :, some_rows(c, 0)], ahead),
            (parts.at[at(3, 1), rows, :, some_rows(c, 1)], pp.at[1, rows, :, some_rows(c, 1)], behind),
            (parts.at[at(2, 0), rows, 0], hh.at[0, rows], ahead),
            (parts.at[at(2, 0), rows, 1], hh.at[1, rows], behind),
            (parts.at[at(1, 0), rows], tt.at[0, rows], ahead),
            (parts.at[at(3, 0), rows], tt.at[1, rows], behind),
            (parts.at[at(0, 1), rows], yb.at[rows], across),
            (parts.at[at(1 if c % 2 == 0 else 3, 1), rows, :, pl.ds(0, 16)], yc.at[rows], across),
        )[i]
        return remote(src, dst, rd_ss.at[c, i], rd_rs.at[c, i], where)

    def sum_first(c):
        for i in (0, 1, 2, 8):
            sum_copy(c, i).start()

    def sum_second(c):
        rows = span(c)
        sum_copy(c, 0).wait_recv()
        far = at(2, 0)
        parts[far, rows] = (f32(parts[far, rows]) + f32(ya[rows])).astype(bf16)
        sum_copy(c, 3).start()
        sum_copy(c, 4).start()

    def sum_third(c):
        rows = span(c)
        sum_copy(c, 1).wait_recv()
        sum_copy(c, 2).wait_recv()
        other, short = at(0, 1), c % 2
        few, most = pl.ds(0, 16), pl.ds(16, 48)
        parts[other, rows, :, few] = (
            f32(parts[other, rows, :, few]) + f32(pp[1 - short, rows, :, few])
        ).astype(bf16)
        parts[other, rows, :, most] = (
            f32(parts[other, rows, :, most])
            + f32(pp[0, rows, :, most])
            + f32(pp[1, rows, :, most])
        ).astype(bf16)
        sum_copy(c, 7).start()

    def sum_fourth(c):
        rows, few = span(c), pl.ds(0, 16)
        sum_copy(c, 8).wait_recv()
        near = at(1 if c % 2 == 0 else 3, 0)
        parts[near, rows, :, few] = (f32(parts[near, rows, :, few]) + f32(yc[rows])).astype(bf16)
        for way in range(2):
            sum_copy(c, 3 + way).wait_recv()
            near = at(1 if way == 0 else 3, 0)
            parts[near, rows, way] = (f32(parts[near, rows, way]) + f32(hh[way, rows])).astype(bf16)
            sum_copy(c, 5 + way).start()

    def sum_last(c):
        rows = span(c)
        for i in (5, 6, 7):
            sum_copy(c, i).wait_recv()
        return (f32(parts[me, rows]) + f32(tt[0, rows])) + (f32(tt[1, rows]) + f32(yb[rows]))

    def experts(c):
        rows = span(c)
        count = CHUNKS[c][1] - CHUNKS[c][0]
        height = count * 64
        for e in range(2):
            square = jnp.zeros((height, 1), jnp.float32)
            for f in range(8):
                piece = f32(agb[f, rows, e].reshape(height, 256))
                square = square + jnp.sum(piece * piece, axis=1, keepdims=True)
            scale = lax.rsqrt(square * (1.0 / 2048) + EPSILON)
            for f in range(8):
                cols = slice(f * 256, (f + 1) * 256)
                piece = f32(agb[f, rows, e].reshape(height, 256))
                normed[e, :height, cols] = (piece * scale * gain_ref[:, cols]).astype(bf16)
            lifted = lax.dot_general(
                normed[e, :height, :], up[e], (((1,), (1,)), ((), ())),
                preferred_element_type=jnp.float32,
            )
            gated = lax.dot_general(
                normed[e, :height, :], gate[e], (((1,), (1,)), ((), ())),
                preferred_element_type=jnp.float32,
            )
            hidden = (gated / (1.0 + jnp.exp(-gated)) * lifted).astype(bf16)
            for f in range(8):
                parts[f, rows, e] = jnp.dot(
                    hidden, down[e, :, f * 256 : (f + 1) * 256],
                    preferred_element_type=jnp.float32,
                ).astype(bf16).reshape(count, 64, 256)

    def finish(c):
        rows = span(c)
        count = CHUNKS[c][1] - CHUNKS[c][0]
        fin[rows] = sum_last(c).astype(bf16).reshape(count, 2, 4, 16, 256)
        for slot in remote_slots(c):
            back_copy(*slot).start()
        if c == 0:
            back[ctx] = fin[0, :, 0]

    steps = (
        gather_first, gather_second, gather_third, gather_last, experts,
        sum_first, sum_second, sum_third, sum_fourth, finish,
    )
    ready = False
    for step, c in ORDER:
        if steps[step] is experts and not ready:
            for load in loads:
                load.wait()
            ready = True
        steps[step](c)

    for n, dl in slots[1:]:
        dst = back.at[ctx_at(Z_ORDER[n], dl)]
        remote(dst, dst, f_ss.at[n, dl], f_rs.at[n, dl], across).wait_recv()
    for rows in (slice(0, 256), slice(256, 512)):
        moved = jnp.dot(
            unpack[rows, :], back[...].reshape(1024, 256), preferred_element_type=jnp.float32
        )
        out_ref[rows, :] = (f32(stream[rows, :]) + moved).astype(bf16)

    def drain(t, unused):
        for p in range(2):
            right_copy(t, p).wait_send()
            left_copy(t, p).wait_send()
        sibling_copy(0, t).wait_send()
        sibling_copy(1, t).wait_send()
        return unused

    lax.fori_loop(0, 7, drain, 0)
    for copy in kv_copies + [query_copy, out_copy, near_copy, far_copy]:
        copy.wait_send()
    for i in range(7):
        wo_copy(i).wait_send()
    for c in range(2):
        for i in range(8):
            spread_copy(c, i).wait_send()
    for c in range(len(CHUNKS)):
        for i in range(9):
            sum_copy(c, i).wait_send()
            gather_copy(c, i).wait_send()
    for slot in slots[1:]:
        send_copy(*slot).wait_send()
        back_copy(*slot).wait_send()


def layer(q, k, v, out_weight, residual, gain, ids, gate, up, down):
    rows, width = residual.shape
    dma = pltpu.SemaphoreType.DMA
    vmem, hbm = pl.BlockSpec(memory_space=pltpu.VMEM), pl.BlockSpec(memory_space=pl.ANY)
    bf16, single = jnp.bfloat16, jnp.float32
    pairs = [(7, 2), (7, 2), (2, 7), (6,), (7,)]
    sems = [dma(shape) for shape in pairs for _ in range(2)]
    return pl.pallas_call(
        fused_kernel,
        out_shape=jax.ShapeDtypeStruct((rows, width), bf16),
        in_specs=[vmem] * 7 + [hbm] * 3,
        out_specs=vmem,
        scratch_shapes=[
            pltpu.VMEM((1024, HEAD_DIM), bf16),
            pltpu.VMEM((512, HEAD_DIM), bf16),
            pltpu.VMEM((2, 8, 2, 2, 4, 128, 128), bf16),
            pltpu.VMEM((2, 4, 128, 128), bf16),
            pltpu.VMEM((1024, 2 * HEAD_DIM), single),
            pltpu.VMEM((1024, HEAD_DIM), single),
            pltpu.VMEM((512, HEAD_DIM), bf16),
            pltpu.VMEM((2, 8, 512, HEAD_DIM), bf16),
            pltpu.VMEM((8, 256, 256), bf16),
            pltpu.VMEM(gate.shape, bf16),
            pltpu.VMEM(up.shape, bf16),
            pltpu.VMEM(down.shape, bf16),
            pltpu.VMEM((1024, 512), bf16),
            pltpu.VMEM((512, 1024), bf16),
            pltpu.VMEM((512, 256), bf16),
            pltpu.VMEM((32, 2, 16, 256), bf16),
            pltpu.VMEM((8, 8, 2, 4, 16, 256), bf16),
            pltpu.VMEM((2, 128, 2048), bf16),
            pltpu.VMEM((32, 2, 16, 256), bf16),
            pltpu.VMEM((8, 2, 4, 16, 256), bf16),
            pltpu.VMEM((8, 8, 2, 64, 256), bf16),
            pltpu.VMEM((8, 2, 64, 256), bf16),
            pltpu.VMEM((2, 8, 2, 64, 256), bf16),
            pltpu.VMEM((2, 8, 64, 256), bf16),
            pltpu.VMEM((2, 8, 2, 64, 256), bf16),
            pltpu.VMEM((8, 2, 64, 256), bf16),
            pltpu.VMEM((8, 2, 16, 256), bf16),
        ]
        + sems
        + [dma((3,)), dma((2, 8)), dma((2, 8))]
        + [dma((len(CHUNKS), 9)) for _ in range(4)]
        + [dma((8, 4)) for _ in range(4)],
        compiler_params=pltpu.CompilerParams(
            collective_id=0, has_side_effects=True, vmem_limit_bytes=VMEM_BYTES
        ),
        cost_estimate=pl.CostEstimate(
            flops=15 * 10**9, bytes_accessed=10**7, transcendentals=512 * 16384 * 2
        ),
    )(q, k, v, out_weight, residual, gain, ids, gate, up, down)


def per_device(
    residual,
    query_vectors,
    key_vectors,
    value_vectors,
    out_weight,
    norm_gain,
    species,
    gate_weight,
    up_weight,
    down_weight,
):
    return layer(
        query_vectors, key_vectors, value_vectors, out_weight, residual, norm_gain.reshape(1, -1),
        species.reshape(1, -1), jnp.swapaxes(gate_weight, 1, 2), jnp.swapaxes(up_weight, 1, 2), down_weight,
    )


def solution(mesh):
    return jax.shard_map(
        per_device,
        mesh=mesh,
        in_specs=(
            P("ctx", "exp"),
            P("ctx", "exp"),
            P("ctx", "exp"),
            P("ctx", "exp"),
            P("exp", None),
            P(),
            P("ctx", None),
            P("ctx", None, "exp"),
            P("ctx", None, "exp"),
            P("ctx", "exp", None),
        ),
        out_specs=P("ctx", "exp"),
        check_vma=False,
    )
```

```python
import functools
import math

import jax
import jax.numpy as jnp
from jax import lax
from jax.experimental import pallas as pl
from jax.experimental.pallas import tpu as pltpu
from jax.sharding import PartitionSpec as P

HEAD_DIM = 128
BLK = 8
MOST = 2
EPSILON = 1e-06
EXP2_FACTOR = math.log2(math.e) / math.sqrt(HEAD_DIM)
VMEM_BYTES = 60 * 1024 * 1024
TILE_Q = 512
Z_ORDER = (0, 1, 7, 2, 6, 3, 5, 4)
CHUNKS = ((0, 1), (1, 2), (2, 4), (4, 6), (6, 7), (7, 8))
ORDER = (
    (0, 0), (0, 1), (10, 0), (1, 0), (1, 1), (10, 1), (0, 2), (2, 0), (2, 1), (0, 3),
    (1, 2), (0, 4), (3, 1), (3, 0), (0, 5), (1, 3), (4, 0), (10, 2), (10, 3), (2, 2),
    (5, 0), (4, 1), (2, 3), (1, 4), (10, 4), (3, 2), (5, 1), (1, 5), (6, 0), (4, 2),
    (10, 5), (5, 2), (3, 3), (4, 3), (6, 1), (2, 4), (7, 0), (5, 3), (2, 5), (8, 0),
    (6, 2), (3, 4), (4, 4), (7, 1), (8, 1), (5, 4), (6, 3), (7, 2), (9, 0), (8, 2),
    (3, 5), (4, 5), (6, 4), (5, 5), (7, 3), (8, 3), (7, 4), (9, 2), (9, 1), (6, 5),
    (7, 5), (8, 4), (9, 3), (8, 5), (9, 4), (9, 5),
)
MESH = pl.DeviceIdType.MESH


def remote(src, dst, send_sem, recv_sem, where):
    return pltpu.make_async_remote_copy(
        src_ref=src,
        dst_ref=dst,
        send_sem=send_sem,
        recv_sem=recv_sem,
        device_id=where,
        device_id_type=MESH,
    )


def greet(others):
    barrier = pltpu.get_barrier_semaphore()
    for where in others:
        pl.semaphore_signal(barrier, inc=1, device_id=where, device_id_type=MESH)


def f32(value):
    return value.astype(jnp.float32)


def fused_kernel(
    q_ref, k_ref, v_ref, wo_ref, res_ref, gain_ref, ids_ref, gate_hbm, up_hbm, down_hbm,
    out_ref,
    qbuf, q_give, kv, kv_give, acc, top, o_send, att, wo_cols,
    gate, up, down, pack, unpack, stream, packed, agb, normed, back, fin,
    parts, ya, pp, hh, tt, yb, yc,
    r_ss, r_rs, l_ss, l_rs, s_ss, s_rs, x_ss, x_rs, wo_ss, wo_rs, w_sem, a1_ss, a1_rs,
    rd_ss, rd_rs, ag_ss, ag_rs, b_ss, b_rs, f_ss, f_rs,
):
    ctx = lax.axis_index("ctx")
    z, lane = ctx // 4, ctx % 4
    exp = lax.axis_index("exp")
    x, y = exp % 4, exp // 4
    bf16 = jnp.bfloat16

    def at(dx, dy):
        return ((y + dy) % 2) * 4 + (x + dx) % 4

    def ctx_at(dz, dl):
        return ((z + dz) % 8) * 4 + (lane + dl) % 4

    me = at(0, 0)
    ahead, behind, across = {"exp": at(1, 0)}, {"exp": at(3, 0)}, {"exp": at(0, 1)}
    right, left = {"ctx": ctx_at(1, 0)}, {"ctx": ctx_at(7, 0)}
    sibling = {"ctx": z * 4 + (lane // 2) * 2 + (lane + 1) % 2}
    partner = {"ctx": ctx_at(0, 2)}

    exp_peers = [(dx, dy) for dy in range(2) for dx in range(4) if dx or dy]
    peers = [{"ctx": ctx_at(dz, dl)} for dz in range(8) for dl in range(4) if dz or dl]
    peers += [{"exp": at(dx, dy)} for dx, dy in exp_peers]
    greet(peers)
    loads = [
        pltpu.make_async_copy(src, dst, w_sem.at[i])
        for i, (src, dst) in enumerate(((gate_hbm, gate), (up_hbm, up), (down_hbm, down)))
    ]
    for load in loads:
        load.start()

    head, far_head = lane // 2, 1 - lane // 2
    mine = pl.ds(pl.multiple_of(head * HEAD_DIM, HEAD_DIM), HEAD_DIM)
    theirs = pl.ds(pl.multiple_of(far_head * HEAD_DIM, HEAD_DIM), HEAD_DIM)
    for place, cols in ((kv.at[0, 0, 0], mine), (kv_give, theirs)):
        for j in range(4):
            rows = slice(j * 128, (j + 1) * 128)
            place[0, j] = k_ref[rows, cols].T
            place[1, j] = v_ref[rows, cols]
    qbuf[0:512] = q_ref[:, mine]
    q_give[...] = q_ref[:, theirs]

    pl.semaphore_wait(pltpu.get_barrier_semaphore(), len(peers))

    def right_item(t):
        return 1 + t // 2, t % 2

    def left_item(t):
        return 7 - t // 2, t % 2 + t // 6

    def right_copy(t, p):
        slot, part = right_item(t)
        return remote(
            kv.at[0, slot - 1, part, p], kv.at[0, slot, part, p], r_ss.at[t, p], r_rs.at[t, p], right
        )

    def left_copy(t, p):
        slot, part = left_item(t)
        return remote(
            kv.at[0, (slot + 1) % 8, part, p],
            kv.at[0, slot, part, p],
            l_ss.at[t, p],
            l_rs.at[t, p],
            left,
        )

    def sibling_copy(way, t):
        slot, part = (right_item, left_item)[way](t)
        return remote(
            kv.at[0, slot, part], kv.at[1, slot, part], s_ss.at[way, t], s_rs.at[way, t], sibling
        )

    kv_copies = [
        remote(kv_give.at[p], kv.at[0, 0, 1, p], x_ss.at[p], x_rs.at[p], partner) for p in range(2)
    ]
    query_copy = remote(q_give, qbuf.at[pl.ds(512, 512)], x_ss.at[2], x_rs.at[2], partner)
    out_copy = remote(o_send, att.at[1, me], x_ss.at[3], x_rs.at[3], partner)
    near_copy = remote(kv.at[0, 0, 0], kv.at[1, 0, 0], x_ss.at[4], x_rs.at[4], sibling)
    far_copy = remote(kv.at[0, 0, 1], kv.at[1, 0, 1], x_ss.at[5], x_rs.at[5], sibling)
    for p in range(2):
        right_copy(0, p).start()
        left_copy(0, p).start()
        kv_copies[p].start()
    near_copy.start()
    query_copy.start()

    def wo_block(index):
        return pl.ds(pl.multiple_of(index * 256, 256), 256)

    def wo_copy(i):
        dx, dy = exp_peers[i]
        to = at(dx, dy)
        return remote(
            wo_ref.at[:, wo_block(to)], wo_cols.at[me], wo_ss.at[i], wo_rs.at[i], {"exp": to}
        )

    acc[...] = jnp.zeros_like(acc)
    top[...] = jnp.full_like(top, -1e30)
    ones = jnp.ones((512, HEAD_DIM), bf16)

    def attend(first, count, chunks):
        def one_tile(index, unused):
            rows = pl.ds(pl.multiple_of(first + index * TILE_Q, TILE_Q), TILE_Q)
            q = qbuf[rows, :]
            scores = [
                jnp.dot(
                    q,
                    jnp.concatenate([kv[kind, slot, part, 0, j] for j in range(4)], axis=1),
                    preferred_element_type=jnp.float32,
                )
                for kind, slot, part in chunks
            ]
            before = top[rows, :]
            best = functools.reduce(jnp.maximum, scores)
            best = jnp.maximum(best[:, :256], best[:, 256:])
            best = jnp.maximum(best[:, :128], best[:, 128:])
            now = jnp.maximum(before, jnp.max(best, axis=1, keepdims=True))
            top[rows, :] = now
            wide_now = jnp.concatenate([now] * 4, axis=1)
            total = None
            for s, (kind, slot, part) in zip(scores, chunks):
                weights = jnp.exp2((s - wide_now) * EXP2_FACTOR).astype(bf16)
                wide = jnp.concatenate([kv[kind, slot, part, 1].reshape(512, 128), ones], axis=1)
                term = jnp.dot(weights, wide, preferred_element_type=jnp.float32)
                total = term if total is None else total + term
            shrink = jnp.exp2((before - now) * EXP2_FACTOR)
            acc[rows, :] = acc[rows, :] * jnp.concatenate([shrink, shrink], axis=1) + total
            return unused

        lax.fori_loop(0, count // TILE_Q, one_tile, 0)

    attend(0, 512, [(0, 0, 0)])
    near_copy.wait_recv()
    attend(0, 512, [(1, 0, 0)])
    def counter(shape, dim):
        return lax.broadcasted_iota(jnp.int32, shape, dim)

    def flag(condition):
        return jnp.where(condition, 1.0, 0.0)

    ids = jnp.broadcast_to(f32(ids_ref[...]), (64, 64))
    ids_t = ids.T
    same = flag(ids == ids_t)
    before_row = flag(counter((64, 64), 0) < counter((64, 64), 1))
    before_col = flag(counter((64, 64), 1) < counter((64, 64), 0))
    slot_row = MOST * ids[0:1, :] + jnp.sum(same * before_row, axis=0, keepdims=True)
    slot_col = MOST * ids_t[:, 0:1] + jnp.sum(same * before_col, axis=1, keepdims=True)
    spans = flag(counter((64, 512), 1) // BLK == counter((64, 512), 0)).astype(bf16)
    spans_t = flag(counter((512, 64), 0) // BLK == counter((512, 64), 1)).astype(bf16)
    token_row = jnp.dot(
        jnp.broadcast_to(slot_row, (8, 64)).astype(bf16), spans, preferred_element_type=jnp.float32
    ).astype(jnp.int32)[0:1, :] * BLK + counter((1, 512), 1) % BLK
    token_col = jnp.dot(
        spans_t, jnp.broadcast_to(slot_col, (64, 128)).astype(bf16),
        preferred_element_type=jnp.float32,
    ).astype(jnp.int32) * BLK + counter((512, 128), 0) % BLK
    for part in range(4):
        places = counter((256, 512), 0) + part * 256
        pack[part * 256 : (part + 1) * 256, :] = flag(places == token_row).astype(bf16)
    for part in range(8):
        places = counter((512, 128), 1) + part * 128
        unpack[:, part * 128 : (part + 1) * 128] = flag(places == token_col).astype(bf16)
    for p in range(2):
        kv_copies[p].wait_recv()
        right_copy(1, p).start()
        left_copy(1, p).start()
    far_copy.start()
    attend(0, 512, [(0, 0, 1)])
    for i in range(7):
        wo_copy(i).start()
    wo_cols[me] = wo_ref[:, wo_block(me)]

    def pass_on(t):
        for p in range(2):
            right_copy(t, p).wait_recv()

            @pl.when(t < 5)
            def _():
                right_copy(t + 2, p).start()

            left_copy(t, p).wait_recv()

            @pl.when(t < 4)
            def _():
                left_copy(t + 2, p).start()

            @pl.when(t == 5)
            def _():
                left_copy(6, p).start()

        sibling_copy(0, t).start()
        sibling_copy(1, t).start()

    def stage(t, unused):
        pass_on(t)

        @pl.when(t == 0)
        def _():
            query_copy.wait_recv()
            far_copy.wait_recv()

        @pl.when(t < 5)
        def _():
            attend(512 * (1 - t // 4), 512, [(t % 2 + t // 4, 0, t // 2 - t // 4)])

        attend(0, 1024, [(0,) + right_item(t), (0,) + left_item(t)])
        sibling_copy(0, t).wait_recv()
        sibling_copy(1, t).wait_recv()
        attend(0, 1024, [(1,) + right_item(t), (1,) + left_item(t)])
        return unused

    lax.fori_loop(0, 6, stage, 0)

    def many(c, way):
        return pl.ds(128, 384) if c == way else pl.ds(0, 512)

    def spread_copy(c, i):
        low, high = pl.ds(0, 256), pl.ds(256, 256)
        src, where = (
            (att.at[c, me], across),
            (att.at[c, me], ahead),
            (att.at[c, me], behind),
            (att.at[c, at(0, 1), many(c, 0)], ahead),
            (att.at[c, at(0, 1), many(c, 1)], behind),
            (att.at[c, at(3, 0), low], ahead),
            (att.at[c, at(1, 0), high], behind),
            (att.at[c, at(2, 0)], across),
            (att.at[c, at(3 if c == 0 else 1, 0), pl.ds(0, 128)], across),
        )[i]
        return remote(src, src, a1_ss.at[c, i], a1_rs.at[c, i], where)

    def spread_landed(c, i):
        low, high = pl.ds(0, 256), pl.ds(256, 256)
        dst = (
            att.at[c, at(0, 1)],
            att.at[c, at(3, 0)],
            att.at[c, at(1, 0)],
            att.at[c, at(3, 1), many(c, 0)],
            att.at[c, at(1, 1), many(c, 1)],
            att.at[c, at(2, 0), low],
            att.at[c, at(2, 0), high],
            att.at[c, at(2, 1)],
            att.at[c, at(3 if c == 0 else 1, 1), pl.ds(0, 128)],
        )[i]
        remote(dst, dst, a1_ss.at[c, i], a1_rs.at[c, i], across).wait_recv()

    pass_on(6)
    attend(0, 512, [(0, 4, 0), (0, 4, 1)])
    sibling_copy(0, 6).wait_recv()
    sibling_copy(1, 6).wait_recv()
    attend(0, 512, [(1, 4, 0), (1, 4, 1)])
    att[0, me] = (acc[:512, :HEAD_DIM] / acc[:512, HEAD_DIM:]).astype(bf16)
    for i in range(3):
        spread_copy(0, i).start()
    attend(512, 512, [(0, 4, 0), (0, 4, 1)])
    attend(512, 512, [(1, 4, 0), (1, 4, 1)])
    o_send[...] = (acc[512:, :HEAD_DIM] / acc[512:, HEAD_DIM:]).astype(bf16)
    out_copy.start()
    for c in range(2):
        if c == 1:
            out_copy.wait_recv()
            for i in range(3):
                spread_copy(1, i).start()
        for i, nexts in ((1, (5,)), (2, (6, 8)), (0, (3, 4))):
            spread_landed(c, i)
            for n in nexts:
                spread_copy(c, n).start()
    for c in range(2):
        spread_landed(c, 5)
        spread_landed(c, 6)
        spread_copy(c, 7).start()
    for i in range(7):
        dx, dy = exp_peers[i]
        dst = wo_cols.at[at(4 - dx, dy)]
        remote(dst, dst, wo_ss.at[i], wo_rs.at[i], across).wait_recv()
    for c in range(2):
        for i in (3, 4, 7, 8):
            spread_landed(c, i)
    near_rows, far_rows = mine, theirs
    for part in range(2):
        rows = slice(part * 256, (part + 1) * 256)
        total = f32(res_ref[rows, :])
        for f in range(8):
            total = total + jnp.dot(
                jnp.concatenate([att[0, f, rows, :], att[1, f, rows, :]], axis=1),
                jnp.concatenate([wo_cols[f, near_rows, :], wo_cols[f, far_rows, :]], axis=0),
                preferred_element_type=jnp.float32,
            )
        stream[rows, :] = total.astype(bf16)

    slots = [(n, dl) for n in range(8) for dl in range(4)]

    def remote_slots(c):
        return [s for s in slots if s[0] in range(*CHUNKS[c]) and s != (0, 0)]

    def send_copy(n, dl):
        to = ctx_at(Z_ORDER[n], dl)
        return remote(
            packed.at[to], agb.at[me, n, :, dl], b_ss.at[n, dl], b_rs.at[n, dl], {"ctx": to}
        )

    def back_copy(n, dl):
        to = ctx_at(8 - Z_ORDER[n], 4 - dl)
        return remote(
            fin.at[n, :, dl], back.at[ctx], f_ss.at[n, dl], f_rs.at[n, dl], {"ctx": to}
        )

    for part in range(4):
        packed[part * 8 : (part + 1) * 8] = jnp.dot(
            pack[part * 256 : (part + 1) * 256, :], stream[...],
            preferred_element_type=jnp.float32,
        ).astype(bf16).reshape(8, 2, 16, 256)
    for c in range(len(CHUNKS)):
        for slot in remote_slots(c):
            send_copy(*slot).start()
    agb[me, 0, :, 0] = packed[ctx]

    def span(c):
        return pl.ds(CHUNKS[c][0], CHUNKS[c][1] - CHUNKS[c][0])

    def some(c, way):
        return pl.ds(1, 3) if c % 2 == way else pl.ds(0, 4)

    def some_rows(c, way):
        return pl.ds(16, 48) if c % 2 == way else pl.ds(0, 64)

    def gather_copy(c, i):
        rows = span(c)
        src, where = (
            (agb.at[me, rows], across),
            (agb.at[me, rows], ahead),
            (agb.at[me, rows], behind),
            (agb.at[at(0, 1), rows, :, some(c, 0)], ahead),
            (agb.at[at(0, 1), rows, :, some(c, 1)], behind),
            (agb.at[at(3, 0), rows, 0], ahead),
            (agb.at[at(1, 0), rows, 1], behind),
            (agb.at[at(2, 0), rows], across),
            (agb.at[at(3 if c % 2 == 0 else 1, 0), rows, :, pl.ds(0, 1)], across),
        )[i]
        return remote(src, src, ag_ss.at[c, i], ag_rs.at[c, i], where)

    def gather_first(c):
        for slot in remote_slots(c):
            send_copy(*slot).wait_recv()
        for i in range(3):
            gather_copy(c, i).start()

    def landed(c, i):
        rows = span(c)
        dst = (
            agb.at[at(0, 1), rows],
            agb.at[at(3, 0), rows],
            agb.at[at(1, 0), rows],
            agb.at[at(3, 1), rows, :, some(c, 0)],
            agb.at[at(1, 1), rows, :, some(c, 1)],
            agb.at[at(2, 0), rows, 0],
            agb.at[at(2, 0), rows, 1],
            agb.at[at(2, 1), rows],
            agb.at[at(3 if c % 2 == 0 else 1, 1), rows, :, pl.ds(0, 1)],
        )[i]
        remote(dst, dst, ag_ss.at[c, i], ag_rs.at[c, i], across).wait_recv()

    def gather_near(c):
        landed(c, 0)
        gather_copy(c, 3).start()
        gather_copy(c, 4).start()

    def gather_second(c):
        landed(c, 1)
        gather_copy(c, 5).start()
        landed(c, 2)
        gather_copy(c, 6).start()
        gather_copy(c, 8).start()

    def gather_third(c):
        landed(c, 5)
        landed(c, 6)
        gather_copy(c, 7).start()

    def gather_last(c):
        for i in (3, 4, 7, 8):
            landed(c, i)

    def sum_copy(c, i):
        rows = span(c)
        src, dst, where = (
            (parts.at[at(2, 1), rows], ya.at[rows], across),
            (parts.at[at(1, 1), rows, :, some_rows(c, 0)], pp.at[0, rows, :, some_rows(c, 0)], ahead),
            (parts.at[at(3, 1), rows, :, some_rows(c, 1)], pp.at[1, rows, :, some_rows(c, 1)], behind),
            (parts.at[at(2, 0), rows, 0], hh.at[0, rows], ahead),
            (parts.at[at(2, 0), rows, 1], hh.at[1, rows], behind),
            (parts.at[at(1, 0), rows], tt.at[0, rows], ahead),
            (parts.at[at(3, 0), rows], tt.at[1, rows], behind),
            (parts.at[at(0, 1), rows], yb.at[rows], across),
            (parts.at[at(1 if c % 2 == 0 else 3, 1), rows, :, pl.ds(0, 16)], yc.at[rows], across),
        )[i]
        return remote(src, dst, rd_ss.at[c, i], rd_rs.at[c, i], where)

    def sum_first(c):
        for i in (0, 1, 2, 8):
            sum_copy(c, i).start()

    def sum_second(c):
        rows = span(c)
        sum_copy(c, 0).wait_recv()
        far = at(2, 0)
        parts[far, rows] = (f32(parts[far, rows]) + f32(ya[rows])).astype(bf16)
        sum_copy(c, 3).start()
        sum_copy(c, 4).start()

    def sum_third(c):
        rows = span(c)
        sum_copy(c, 1).wait_recv()
        sum_copy(c, 2).wait_recv()
        other, short = at(0, 1), c % 2
        few, most = pl.ds(0, 16), pl.ds(16, 48)
        parts[other, rows, :, few] = (
            f32(parts[other, rows, :, few]) + f32(pp[1 - short, rows, :, few])
        ).astype(bf16)
        parts[other, rows, :, most] = (
            f32(parts[other, rows, :, most])
            + f32(pp[0, rows, :, most])
            + f32(pp[1, rows, :, most])
        ).astype(bf16)
        sum_copy(c, 7).start()

    def sum_fourth(c):
        rows, few = span(c), pl.ds(0, 16)
        sum_copy(c, 8).wait_recv()
        near = at(1 if c % 2 == 0 else 3, 0)
        parts[near, rows, :, few] = (f32(parts[near, rows, :, few]) + f32(yc[rows])).astype(bf16)
        for way in range(2):
            sum_copy(c, 3 + way).wait_recv()
            near = at(1 if way == 0 else 3, 0)
            parts[near, rows, way] = (f32(parts[near, rows, way]) + f32(hh[way, rows])).astype(bf16)
            sum_copy(c, 5 + way).start()

    def sum_last(c):
        rows = span(c)
        for i in (5, 6, 7):
            sum_copy(c, i).wait_recv()
        return (f32(parts[me, rows]) + f32(tt[0, rows])) + (f32(tt[1, rows]) + f32(yb[rows]))

    def experts(c):
        rows = span(c)
        count = CHUNKS[c][1] - CHUNKS[c][0]
        height = count * 64
        for e in range(2):
            square = jnp.zeros((height, 1), jnp.float32)
            for f in range(8):
                piece = f32(agb[f, rows, e].reshape(height, 256))
                square = square + jnp.sum(piece * piece, axis=1, keepdims=True)
            scale = lax.rsqrt(square * (1.0 / 2048) + EPSILON)
            for f in range(8):
                cols = slice(f * 256, (f + 1) * 256)
                piece = f32(agb[f, rows, e].reshape(height, 256))
                normed[e, :height, cols] = (piece * scale * gain_ref[:, cols]).astype(bf16)
            lifted = lax.dot_general(
                normed[e, :height, :], up[e], (((1,), (1,)), ((), ())),
                preferred_element_type=jnp.float32,
            )
            gated = lax.dot_general(
                normed[e, :height, :], gate[e], (((1,), (1,)), ((), ())),
                preferred_element_type=jnp.float32,
            )
            hidden = (gated / (1.0 + jnp.exp(-gated)) * lifted).astype(bf16)
            for f in range(8):
                parts[f, rows, e] = jnp.dot(
                    hidden, down[e, :, f * 256 : (f + 1) * 256],
                    preferred_element_type=jnp.float32,
                ).astype(bf16).reshape(count, 64, 256)

    def finish(c):
        rows = span(c)
        count = CHUNKS[c][1] - CHUNKS[c][0]
        fin[rows] = sum_last(c).astype(bf16).reshape(count, 2, 4, 16, 256)
        for slot in remote_slots(c):
            back_copy(*slot).start()
        if c == 0:
            back[ctx] = fin[0, :, 0]

    steps = (
        gather_first, gather_second, gather_third, gather_last, experts,
        sum_first, sum_second, sum_third, sum_fourth, finish, gather_near,
    )
    ready = False
    for step, c in ORDER:
        if steps[step] is experts and not ready:
            for load in loads:
                load.wait()
            ready = True
        steps[step](c)

    for n, dl in slots[1:]:
        dst = back.at[ctx_at(Z_ORDER[n], dl)]
        remote(dst, dst, f_ss.at[n, dl], f_rs.at[n, dl], across).wait_recv()
    for rows in (slice(0, 256), slice(256, 512)):
        moved = jnp.dot(
            unpack[rows, :], back[...].reshape(1024, 256), preferred_element_type=jnp.float32
        )
        out_ref[rows, :] = (f32(stream[rows, :]) + moved).astype(bf16)

    def drain(t, unused):
        for p in range(2):
            right_copy(t, p).wait_send()
            left_copy(t, p).wait_send()
        sibling_copy(0, t).wait_send()
        sibling_copy(1, t).wait_send()
        return unused

    lax.fori_loop(0, 7, drain, 0)
    for copy in kv_copies + [query_copy, out_copy, near_copy, far_copy]:
        copy.wait_send()
    for i in range(7):
        wo_copy(i).wait_send()
    for c in range(2):
        for i in range(9):
            spread_copy(c, i).wait_send()
    for c in range(len(CHUNKS)):
        for i in range(9):
            sum_copy(c, i).wait_send()
            gather_copy(c, i).wait_send()
    for slot in slots[1:]:
        send_copy(*slot).wait_send()
        back_copy(*slot).wait_send()


def layer(q, k, v, out_weight, residual, gain, ids, gate, up, down):
    rows, width = residual.shape
    dma = pltpu.SemaphoreType.DMA
    vmem, hbm = pl.BlockSpec(memory_space=pltpu.VMEM), pl.BlockSpec(memory_space=pl.ANY)
    bf16, single = jnp.bfloat16, jnp.float32
    pairs = [(7, 2), (7, 2), (2, 7), (6,), (7,)]
    sems = [dma(shape) for shape in pairs for _ in range(2)]
    return pl.pallas_call(
        fused_kernel,
        out_shape=jax.ShapeDtypeStruct((rows, width), bf16),
        in_specs=[vmem] * 7 + [hbm] * 3,
        out_specs=vmem,
        scratch_shapes=[
            pltpu.VMEM((1024, HEAD_DIM), bf16),
            pltpu.VMEM((512, HEAD_DIM), bf16),
            pltpu.VMEM((2, 8, 2, 2, 4, 128, 128), bf16),
            pltpu.VMEM((2, 4, 128, 128), bf16),
            pltpu.VMEM((1024, 2 * HEAD_DIM), single),
            pltpu.VMEM((1024, HEAD_DIM), single),
            pltpu.VMEM((512, HEAD_DIM), bf16),
            pltpu.VMEM((2, 8, 512, HEAD_DIM), bf16),
            pltpu.VMEM((8, 256, 256), bf16),
            pltpu.VMEM(gate.shape, bf16),
            pltpu.VMEM(up.shape, bf16),
            pltpu.VMEM(down.shape, bf16),
            pltpu.VMEM((1024, 512), bf16),
            pltpu.VMEM((512, 1024), bf16),
            pltpu.VMEM((512, 256), bf16),
            pltpu.VMEM((32, 2, 16, 256), bf16),
            pltpu.VMEM((8, 8, 2, 4, 16, 256), bf16),
            pltpu.VMEM((2, 128, 2048), bf16),
            pltpu.VMEM((32, 2, 16, 256), bf16),
            pltpu.VMEM((8, 2, 4, 16, 256), bf16),
            pltpu.VMEM((8, 8, 2, 64, 256), bf16),
            pltpu.VMEM((8, 2, 64, 256), bf16),
            pltpu.VMEM((2, 8, 2, 64, 256), bf16),
            pltpu.VMEM((2, 8, 64, 256), bf16),
            pltpu.VMEM((2, 8, 2, 64, 256), bf16),
            pltpu.VMEM((8, 2, 64, 256), bf16),
            pltpu.VMEM((8, 2, 16, 256), bf16),
        ]
        + sems
        + [dma((3,)), dma((2, 9)), dma((2, 9))]
        + [dma((len(CHUNKS), 9)) for _ in range(4)]
        + [dma((8, 4)) for _ in range(4)],
        compiler_params=pltpu.CompilerParams(
            collective_id=0, has_side_effects=True, vmem_limit_bytes=VMEM_BYTES
        ),
        cost_estimate=pl.CostEstimate(
            flops=15 * 10**9, bytes_accessed=10**7, transcendentals=512 * 16384 * 2
        ),
    )(q, k, v, out_weight, residual, gain, ids, gate, up, down)


def per_device(
    residual,
    query_vectors,
    key_vectors,
    value_vectors,
    out_weight,
    norm_gain,
    species,
    gate_weight,
    up_weight,
    down_weight,
):
    return layer(
        query_vectors, key_vectors, value_vectors, out_weight, residual, norm_gain.reshape(1, -1),
        species.reshape(1, -1), jnp.swapaxes(gate_weight, 1, 2), jnp.swapaxes(up_weight, 1, 2), down_weight,
    )


def solution(mesh):
    return jax.shard_map(
        per_device,
        mesh=mesh,
        in_specs=(
            P("ctx", "exp"),
            P("ctx", "exp"),
            P("ctx", "exp"),
            P("ctx", "exp"),
            P("exp", None),
            P(),
            P("ctx", None),
            P("ctx", None, "exp"),
            P("ctx", None, "exp"),
            P("ctx", "exp", None),
        ),
        out_specs=P("ctx", "exp"),
        check_vma=False,
    )
```

```python
import functools
import math

import jax
import jax.numpy as jnp
from jax import lax
from jax.experimental import pallas as pl
from jax.experimental.pallas import tpu as pltpu
from jax.sharding import PartitionSpec as P

HEAD_DIM = 128
BLK = 8
MOST = 2
EPSILON = 1e-06
EXP2_FACTOR = math.log2(math.e) / math.sqrt(HEAD_DIM)
VMEM_BYTES = 60 * 1024 * 1024
TILE_Q = 512
Z_ORDER = (0, 1, 7, 2, 6, 3, 5, 4)
CHUNKS = ((0, 1), (1, 2), (2, 3), (3, 4), (4, 5), (5, 6), (6, 7), (7, 8))
ORDER = (
    (0, 0), (0, 1), (0, 2), (1, 0), (0, 3), (10, 0), (0, 4), (1, 2), (0, 5), (1, 1),
    (1, 3), (10, 1), (2, 0), (0, 6), (10, 2), (1, 4), (2, 2), (10, 5), (3, 0), (1, 5),
    (2, 1), (2, 3), (10, 3), (0, 7), (4, 0), (5, 0), (1, 6), (3, 2), (4, 2), (2, 4),
    (3, 1), (3, 3), (10, 4), (2, 5), (5, 2), (6, 0), (4, 1), (5, 1), (4, 3), (10, 6),
    (2, 6), (7, 0), (3, 4), (1, 7), (10, 7), (4, 4), (5, 3), (6, 2), (6, 1), (3, 5),
    (4, 5), (2, 7), (8, 0), (5, 4), (3, 6), (5, 5), (7, 1), (6, 3), (4, 6), (8, 1),
    (3, 7), (6, 4), (5, 6), (4, 7), (5, 7), (7, 3), (8, 3), (7, 2), (6, 5), (7, 4),
    (7, 5), (9, 0), (8, 2), (6, 6), (9, 1), (8, 4), (9, 3), (6, 7), (8, 5), (7, 6),
    (8, 6), (9, 2), (7, 7), (9, 4), (8, 7), (9, 5), (9, 6), (9, 7),
)
MESH = pl.DeviceIdType.MESH


def remote(src, dst, send_sem, recv_sem, where):
    return pltpu.make_async_remote_copy(
        src_ref=src,
        dst_ref=dst,
        send_sem=send_sem,
        recv_sem=recv_sem,
        device_id=where,
        device_id_type=MESH,
    )


def greet(others):
    barrier = pltpu.get_barrier_semaphore()
    for where in others:
        pl.semaphore_signal(barrier, inc=1, device_id=where, device_id_type=MESH)


def f32(value):
    return value.astype(jnp.float32)


def fused_kernel(
    q_ref, k_ref, v_ref, wo_ref, res_ref, gain_ref, ids_ref, gate_hbm, up_hbm, down_hbm,
    out_ref,
    qbuf, q_give, kv, kv_give, acc, top, o_send, att, wo_cols,
    gate, up, down, pack, unpack, stream, packed, agb, normed, back, fin,
    parts, ya, pp, hh, tt, yb, yc,
    r_ss, r_rs, l_ss, l_rs, s_ss, s_rs, x_ss, x_rs, wo_ss, wo_rs, w_sem, a1_ss, a1_rs,
    rd_ss, rd_rs, ag_ss, ag_rs, b_ss, b_rs, f_ss, f_rs,
):
    ctx = lax.axis_index("ctx")
    z, lane = ctx // 4, ctx % 4
    exp = lax.axis_index("exp")
    x, y = exp % 4, exp // 4
    bf16 = jnp.bfloat16

    def at(dx, dy):
        return ((y + dy) % 2) * 4 + (x + dx) % 4

    def ctx_at(dz, dl):
        return ((z + dz) % 8) * 4 + (lane + dl) % 4

    me = at(0, 0)
    ahead, behind, across = {"exp": at(1, 0)}, {"exp": at(3, 0)}, {"exp": at(0, 1)}
    right, left = {"ctx": ctx_at(1, 0)}, {"ctx": ctx_at(7, 0)}
    sibling = {"ctx": z * 4 + (lane // 2) * 2 + (lane + 1) % 2}
    partner = {"ctx": ctx_at(0, 2)}

    exp_peers = [(dx, dy) for dy in range(2) for dx in range(4) if dx or dy]
    peers = [{"ctx": ctx_at(dz, dl)} for dz in range(8) for dl in range(4) if dz or dl]
    peers += [{"exp": at(dx, dy)} for dx, dy in exp_peers]
    greet(peers)
    loads = [
        pltpu.make_async_copy(src, dst, w_sem.at[i])
        for i, (src, dst) in enumerate(((gate_hbm, gate), (up_hbm, up), (down_hbm, down)))
    ]
    for load in loads:
        load.start()

    head, far_head = lane // 2, 1 - lane // 2
    mine = pl.ds(pl.multiple_of(head * HEAD_DIM, HEAD_DIM), HEAD_DIM)
    theirs = pl.ds(pl.multiple_of(far_head * HEAD_DIM, HEAD_DIM), HEAD_DIM)
    for place, cols in ((kv.at[0, 0, 0], mine), (kv_give, theirs)):
        for j in range(4):
            rows = slice(j * 128, (j + 1) * 128)
            place[0, j] = k_ref[rows, cols].T
            place[1, j] = v_ref[rows, cols]
    qbuf[0:512] = q_ref[:, mine]
    q_give[...] = q_ref[:, theirs]

    pl.semaphore_wait(pltpu.get_barrier_semaphore(), len(peers))

    def right_item(t):
        return 1 + t // 2, t % 2

    def left_item(t):
        return 7 - t // 2, t % 2 + t // 6

    def right_copy(t, p):
        slot, part = right_item(t)
        return remote(
            kv.at[0, slot - 1, part, p], kv.at[0, slot, part, p], r_ss.at[t, p], r_rs.at[t, p], right
        )

    def left_copy(t, p):
        slot, part = left_item(t)
        return remote(
            kv.at[0, (slot + 1) % 8, part, p],
            kv.at[0, slot, part, p],
            l_ss.at[t, p],
            l_rs.at[t, p],
            left,
        )

    def sibling_copy(way, t):
        slot, part = (right_item, left_item)[way](t)
        return remote(
            kv.at[0, slot, part], kv.at[1, slot, part], s_ss.at[way, t], s_rs.at[way, t], sibling
        )

    kv_copies = [
        remote(kv_give.at[p], kv.at[0, 0, 1, p], x_ss.at[p], x_rs.at[p], partner) for p in range(2)
    ]
    query_copy = remote(q_give, qbuf.at[pl.ds(512, 512)], x_ss.at[2], x_rs.at[2], partner)
    out_copy = remote(o_send, att.at[1, me], x_ss.at[3], x_rs.at[3], partner)
    near_copy = remote(kv.at[0, 0, 0], kv.at[1, 0, 0], x_ss.at[4], x_rs.at[4], sibling)
    far_copy = remote(kv.at[0, 0, 1], kv.at[1, 0, 1], x_ss.at[5], x_rs.at[5], sibling)
    for p in range(2):
        right_copy(0, p).start()
        left_copy(0, p).start()
        kv_copies[p].start()
    near_copy.start()
    query_copy.start()

    def wo_block(index):
        return pl.ds(pl.multiple_of(index * 256, 256), 256)

    def wo_copy(i):
        dx, dy = exp_peers[i]
        to = at(dx, dy)
        return remote(
            wo_ref.at[:, wo_block(to)], wo_cols.at[me], wo_ss.at[i], wo_rs.at[i], {"exp": to}
        )

    acc[...] = jnp.zeros_like(acc)
    top[...] = jnp.full_like(top, -1e30)
    ones = jnp.ones((512, HEAD_DIM), bf16)

    def attend(first, count, chunks):
        def one_tile(index, unused):
            rows = pl.ds(pl.multiple_of(first + index * TILE_Q, TILE_Q), TILE_Q)
            q = qbuf[rows, :]
            scores = [
                jnp.dot(
                    q,
                    jnp.concatenate([kv[kind, slot, part, 0, j] for j in range(4)], axis=1),
                    preferred_element_type=jnp.float32,
                )
                for kind, slot, part in chunks
            ]
            before = top[rows, :]
            best = functools.reduce(jnp.maximum, scores)
            best = jnp.maximum(best[:, :256], best[:, 256:])
            best = jnp.maximum(best[:, :128], best[:, 128:])
            now = jnp.maximum(before, jnp.max(best, axis=1, keepdims=True))
            top[rows, :] = now
            wide_now = jnp.concatenate([now] * 4, axis=1)
            total = None
            for s, (kind, slot, part) in zip(scores, chunks):
                weights = jnp.exp2((s - wide_now) * EXP2_FACTOR).astype(bf16)
                wide = jnp.concatenate([kv[kind, slot, part, 1].reshape(512, 128), ones], axis=1)
                term = jnp.dot(weights, wide, preferred_element_type=jnp.float32)
                total = term if total is None else total + term
            shrink = jnp.exp2((before - now) * EXP2_FACTOR)
            acc[rows, :] = acc[rows, :] * jnp.concatenate([shrink, shrink], axis=1) + total
            return unused

        lax.fori_loop(0, count // TILE_Q, one_tile, 0)

    attend(0, 512, [(0, 0, 0)])
    near_copy.wait_recv()
    attend(0, 512, [(1, 0, 0)])
    def counter(shape, dim):
        return lax.broadcasted_iota(jnp.int32, shape, dim)

    def flag(condition):
        return jnp.where(condition, 1.0, 0.0)

    ids = jnp.broadcast_to(f32(ids_ref[...]), (64, 64))
    ids_t = ids.T
    same = flag(ids == ids_t)
    before_row = flag(counter((64, 64), 0) < counter((64, 64), 1))
    before_col = flag(counter((64, 64), 1) < counter((64, 64), 0))
    slot_row = MOST * ids[0:1, :] + jnp.sum(same * before_row, axis=0, keepdims=True)
    slot_col = MOST * ids_t[:, 0:1] + jnp.sum(same * before_col, axis=1, keepdims=True)
    spans = flag(counter((64, 512), 1) // BLK == counter((64, 512), 0)).astype(bf16)
    spans_t = flag(counter((512, 64), 0) // BLK == counter((512, 64), 1)).astype(bf16)
    token_row = jnp.dot(
        jnp.broadcast_to(slot_row, (8, 64)).astype(bf16), spans, preferred_element_type=jnp.float32
    ).astype(jnp.int32)[0:1, :] * BLK + counter((1, 512), 1) % BLK
    token_col = jnp.dot(
        spans_t, jnp.broadcast_to(slot_col, (64, 128)).astype(bf16),
        preferred_element_type=jnp.float32,
    ).astype(jnp.int32) * BLK + counter((512, 128), 0) % BLK
    for part in range(4):
        places = counter((256, 512), 0) + part * 256
        pack[part * 256 : (part + 1) * 256, :] = flag(places == token_row).astype(bf16)
    for part in range(8):
        places = counter((512, 128), 1) + part * 128
        unpack[:, part * 128 : (part + 1) * 128] = flag(places == token_col).astype(bf16)
    for p in range(2):
        kv_copies[p].wait_recv()
        right_copy(1, p).start()
        left_copy(1, p).start()
    far_copy.start()
    attend(0, 512, [(0, 0, 1)])
    for i in range(7):
        wo_copy(i).start()
    wo_cols[me] = wo_ref[:, wo_block(me)]

    def pass_on(t):
        for p in range(2):
            right_copy(t, p).wait_recv()

            @pl.when(t < 5)
            def _():
                right_copy(t + 2, p).start()

            left_copy(t, p).wait_recv()

            @pl.when(t < 4)
            def _():
                left_copy(t + 2, p).start()

            @pl.when(t == 5)
            def _():
                left_copy(6, p).start()

        sibling_copy(0, t).start()
        sibling_copy(1, t).start()

    def stage(t, unused):
        pass_on(t)

        @pl.when(t == 0)
        def _():
            query_copy.wait_recv()
            far_copy.wait_recv()

        @pl.when(t < 5)
        def _():
            attend(512 * (1 - t // 4), 512, [(t % 2 + t // 4, 0, t // 2 - t // 4)])

        attend(0, 1024, [(0,) + right_item(t), (0,) + left_item(t)])
        sibling_copy(0, t).wait_recv()
        sibling_copy(1, t).wait_recv()
        attend(0, 1024, [(1,) + right_item(t), (1,) + left_item(t)])
        return unused

    lax.fori_loop(0, 6, stage, 0)

    def many(c, way):
        return pl.ds(128, 384) if c == way else pl.ds(0, 512)

    def spread_copy(c, i):
        low, high = pl.ds(0, 256), pl.ds(256, 256)
        src, where = (
            (att.at[c, me], across),
            (att.at[c, me], ahead),
            (att.at[c, me], behind),
            (att.at[c, at(0, 1), many(c, 0)], ahead),
            (att.at[c, at(0, 1), many(c, 1)], behind),
            (att.at[c, at(3, 0), low], ahead),
            (att.at[c, at(1, 0), high], behind),
            (att.at[c, at(2, 0)], across),
            (att.at[c, at(3 if c == 0 else 1, 0), pl.ds(0, 128)], across),
        )[i]
        return remote(src, src, a1_ss.at[c, i], a1_rs.at[c, i], where)

    def spread_landed(c, i):
        low, high = pl.ds(0, 256), pl.ds(256, 256)
        dst = (
            att.at[c, at(0, 1)],
            att.at[c, at(3, 0)],
            att.at[c, at(1, 0)],
            att.at[c, at(3, 1), many(c, 0)],
            att.at[c, at(1, 1), many(c, 1)],
            att.at[c, at(2, 0), low],
            att.at[c, at(2, 0), high],
            att.at[c, at(2, 1)],
            att.at[c, at(3 if c == 0 else 1, 1), pl.ds(0, 128)],
        )[i]
        remote(dst, dst, a1_ss.at[c, i], a1_rs.at[c, i], across).wait_recv()

    pass_on(6)
    attend(0, 512, [(0, 4, 0), (0, 4, 1)])
    sibling_copy(0, 6).wait_recv()
    sibling_copy(1, 6).wait_recv()
    attend(0, 512, [(1, 4, 0), (1, 4, 1)])
    att[0, me] = (acc[:512, :HEAD_DIM] / acc[:512, HEAD_DIM:]).astype(bf16)
    for i in range(3):
        spread_copy(0, i).start()
    attend(512, 512, [(0, 4, 0), (0, 4, 1)])
    attend(512, 512, [(1, 4, 0), (1, 4, 1)])
    o_send[...] = (acc[512:, :HEAD_DIM] / acc[512:, HEAD_DIM:]).astype(bf16)
    out_copy.start()
    for c in range(2):
        if c == 1:
            out_copy.wait_recv()
            for i in range(3):
                spread_copy(1, i).start()
        for i, nexts in ((1, (5,)), (2, (6, 8)), (0, (3, 4))):
            spread_landed(c, i)
            for n in nexts:
                spread_copy(c, n).start()
    for c in range(2):
        spread_landed(c, 5)
        spread_landed(c, 6)
        spread_copy(c, 7).start()
    for i in range(7):
        dx, dy = exp_peers[i]
        dst = wo_cols.at[at(4 - dx, dy)]
        remote(dst, dst, wo_ss.at[i], wo_rs.at[i], across).wait_recv()
    for c in range(2):
        for i in (3, 4, 7, 8):
            spread_landed(c, i)
    near_rows, far_rows = mine, theirs
    for part in range(2):
        rows = slice(part * 256, (part + 1) * 256)
        total = f32(res_ref[rows, :])
        for f in range(8):
            total = total + jnp.dot(
                jnp.concatenate([att[0, f, rows, :], att[1, f, rows, :]], axis=1),
                jnp.concatenate([wo_cols[f, near_rows, :], wo_cols[f, far_rows, :]], axis=0),
                preferred_element_type=jnp.float32,
            )
        stream[rows, :] = total.astype(bf16)

    slots = [(n, dl) for n in range(8) for dl in range(4)]

    def remote_slots(c):
        return [s for s in slots if s[0] in range(*CHUNKS[c]) and s != (0, 0)]

    def send_copy(n, dl):
        to = ctx_at(Z_ORDER[n], dl)
        return remote(
            packed.at[to], agb.at[me, n, :, dl], b_ss.at[n, dl], b_rs.at[n, dl], {"ctx": to}
        )

    def back_copy(n, dl):
        to = ctx_at(8 - Z_ORDER[n], 4 - dl)
        return remote(
            fin.at[n, :, dl], back.at[ctx], f_ss.at[n, dl], f_rs.at[n, dl], {"ctx": to}
        )

    for part in range(4):
        packed[part * 8 : (part + 1) * 8] = jnp.dot(
            pack[part * 256 : (part + 1) * 256, :], stream[...],
            preferred_element_type=jnp.float32,
        ).astype(bf16).reshape(8, 2, 16, 256)
    for c in range(len(CHUNKS)):
        for slot in remote_slots(c):
            send_copy(*slot).start()
    agb[me, 0, :, 0] = packed[ctx]

    def span(c):
        return pl.ds(CHUNKS[c][0], CHUNKS[c][1] - CHUNKS[c][0])

    def some(c, way):
        return pl.ds(1, 3) if c % 2 == way else pl.ds(0, 4)

    def some_rows(c, way):
        return pl.ds(16, 48) if c % 2 == way else pl.ds(0, 64)

    def gather_copy(c, i):
        rows = span(c)
        src, where = (
            (agb.at[me, rows], across),
            (agb.at[me, rows], ahead),
            (agb.at[me, rows], behind),
            (agb.at[at(0, 1), rows, :, some(c, 0)], ahead),
            (agb.at[at(0, 1), rows, :, some(c, 1)], behind),
            (agb.at[at(3, 0), rows, 0], ahead),
            (agb.at[at(1, 0), rows, 1], behind),
            (agb.at[at(2, 0), rows], across),
            (agb.at[at(3 if c % 2 == 0 else 1, 0), rows, :, pl.ds(0, 1)], across),
        )[i]
        return remote(src, src, ag_ss.at[c, i], ag_rs.at[c, i], where)

    def gather_first(c):
        for slot in remote_slots(c):
            send_copy(*slot).wait_recv()
        for i in range(3):
            gather_copy(c, i).start()

    def landed(c, i):
        rows = span(c)
        dst = (
            agb.at[at(0, 1), rows],
            agb.at[at(3, 0), rows],
            agb.at[at(1, 0), rows],
            agb.at[at(3, 1), rows, :, some(c, 0)],
            agb.at[at(1, 1), rows, :, some(c, 1)],
            agb.at[at(2, 0), rows, 0],
            agb.at[at(2, 0), rows, 1],
            agb.at[at(2, 1), rows],
            agb.at[at(3 if c % 2 == 0 else 1, 1), rows, :, pl.ds(0, 1)],
        )[i]
        remote(dst, dst, ag_ss.at[c, i], ag_rs.at[c, i], across).wait_recv()

    def gather_near(c):
        landed(c, 0)
        gather_copy(c, 3).start()
        gather_copy(c, 4).start()

    def gather_second(c):
        landed(c, 1)
        gather_copy(c, 5).start()
        landed(c, 2)
        gather_copy(c, 6).start()
        gather_copy(c, 8).start()

    def gather_third(c):
        landed(c, 5)
        landed(c, 6)
        gather_copy(c, 7).start()

    def gather_last(c):
        for i in (3, 4, 7, 8):
            landed(c, i)

    def sum_copy(c, i):
        rows = span(c)
        src, dst, where = (
            (parts.at[at(2, 1), rows], ya.at[rows], across),
            (parts.at[at(1, 1), rows, :, some_rows(c, 0)], pp.at[0, rows, :, some_rows(c, 0)], ahead),
            (parts.at[at(3, 1), rows, :, some_rows(c, 1)], pp.at[1, rows, :, some_rows(c, 1)], behind),
            (parts.at[at(2, 0), rows, 0], hh.at[0, rows], ahead),
            (parts.at[at(2, 0), rows, 1], hh.at[1, rows], behind),
            (parts.at[at(1, 0), rows], tt.at[0, rows], ahead),
            (parts.at[at(3, 0), rows], tt.at[1, rows], behind),
            (parts.at[at(0, 1), rows], yb.at[rows], across),
            (parts.at[at(1 if c % 2 == 0 else 3, 1), rows, :, pl.ds(0, 16)], yc.at[rows], across),
        )[i]
        return remote(src, dst, rd_ss.at[c, i], rd_rs.at[c, i], where)

    def sum_first(c):
        for i in (0, 1, 2, 8):
            sum_copy(c, i).start()

    def sum_second(c):
        rows = span(c)
        sum_copy(c, 0).wait_recv()
        far = at(2, 0)
        parts[far, rows] = (f32(parts[far, rows]) + f32(ya[rows])).astype(bf16)
        sum_copy(c, 3).start()
        sum_copy(c, 4).start()

    def sum_third(c):
        rows = span(c)
        sum_copy(c, 1).wait_recv()
        sum_copy(c, 2).wait_recv()
        other, short = at(0, 1), c % 2
        few, most = pl.ds(0, 16), pl.ds(16, 48)
        parts[other, rows, :, few] = (
            f32(parts[other, rows, :, few]) + f32(pp[1 - short, rows, :, few])
        ).astype(bf16)
        parts[other, rows, :, most] = (
            f32(parts[other, rows, :, most])
            + f32(pp[0, rows, :, most])
            + f32(pp[1, rows, :, most])
        ).astype(bf16)
        sum_copy(c, 7).start()

    def sum_fourth(c):
        rows, few = span(c), pl.ds(0, 16)
        sum_copy(c, 8).wait_recv()
        near = at(1 if c % 2 == 0 else 3, 0)
        parts[near, rows, :, few] = (f32(parts[near, rows, :, few]) + f32(yc[rows])).astype(bf16)
        for way in range(2):
            sum_copy(c, 3 + way).wait_recv()
            near = at(1 if way == 0 else 3, 0)
            parts[near, rows, way] = (f32(parts[near, rows, way]) + f32(hh[way, rows])).astype(bf16)
            sum_copy(c, 5 + way).start()

    def sum_last(c):
        rows = span(c)
        for i in (5, 6, 7):
            sum_copy(c, i).wait_recv()
        return (f32(parts[me, rows]) + f32(tt[0, rows])) + (f32(tt[1, rows]) + f32(yb[rows]))

    def experts(c):
        rows = span(c)
        count = CHUNKS[c][1] - CHUNKS[c][0]
        height = count * 64
        for e in range(2):
            square = jnp.zeros((height, 1), jnp.float32)
            for f in range(8):
                piece = f32(agb[f, rows, e].reshape(height, 256))
                square = square + jnp.sum(piece * piece, axis=1, keepdims=True)
            scale = lax.rsqrt(square * (1.0 / 2048) + EPSILON)
            for f in range(8):
                cols = slice(f * 256, (f + 1) * 256)
                piece = f32(agb[f, rows, e].reshape(height, 256))
                normed[e, :height, cols] = (piece * scale * gain_ref[:, cols]).astype(bf16)
            lifted = lax.dot_general(
                normed[e, :height, :], up[e], (((1,), (1,)), ((), ())),
                preferred_element_type=jnp.float32,
            )
            gated = lax.dot_general(
                normed[e, :height, :], gate[e], (((1,), (1,)), ((), ())),
                preferred_element_type=jnp.float32,
            )
            hidden = (gated / (1.0 + jnp.exp(-gated)) * lifted).astype(bf16)
            for f in range(8):
                parts[f, rows, e] = jnp.dot(
                    hidden, down[e, :, f * 256 : (f + 1) * 256],
                    preferred_element_type=jnp.float32,
                ).astype(bf16).reshape(count, 64, 256)

    def finish(c):
        rows = span(c)
        count = CHUNKS[c][1] - CHUNKS[c][0]
        fin[rows] = sum_last(c).astype(bf16).reshape(count, 2, 4, 16, 256)
        for slot in remote_slots(c):
            back_copy(*slot).start()
        if c == 0:
            back[ctx] = fin[0, :, 0]

    steps = (
        gather_first, gather_second, gather_third, gather_last, experts,
        sum_first, sum_second, sum_third, sum_fourth, finish, gather_near,
    )
    ready = False
    for step, c in ORDER:
        if steps[step] is experts and not ready:
            for load in loads:
                load.wait()
            ready = True
        steps[step](c)

    for n, dl in slots[1:]:
        dst = back.at[ctx_at(Z_ORDER[n], dl)]
        remote(dst, dst, f_ss.at[n, dl], f_rs.at[n, dl], across).wait_recv()
    for rows in (slice(0, 256), slice(256, 512)):
        moved = jnp.dot(
            unpack[rows, :], back[...].reshape(1024, 256), preferred_element_type=jnp.float32
        )
        out_ref[rows, :] = (f32(stream[rows, :]) + moved).astype(bf16)

    def drain(t, unused):
        for p in range(2):
            right_copy(t, p).wait_send()
            left_copy(t, p).wait_send()
        sibling_copy(0, t).wait_send()
        sibling_copy(1, t).wait_send()
        return unused

    lax.fori_loop(0, 7, drain, 0)
    for copy in kv_copies + [query_copy, out_copy, near_copy, far_copy]:
        copy.wait_send()
    for i in range(7):
        wo_copy(i).wait_send()
    for c in range(2):
        for i in range(9):
            spread_copy(c, i).wait_send()
    for c in range(len(CHUNKS)):
        for i in range(9):
            sum_copy(c, i).wait_send()
            gather_copy(c, i).wait_send()
    for slot in slots[1:]:
        send_copy(*slot).wait_send()
        back_copy(*slot).wait_send()


def layer(q, k, v, out_weight, residual, gain, ids, gate, up, down):
    rows, width = residual.shape
    dma = pltpu.SemaphoreType.DMA
    vmem, hbm = pl.BlockSpec(memory_space=pltpu.VMEM), pl.BlockSpec(memory_space=pl.ANY)
    bf16, single = jnp.bfloat16, jnp.float32
    pairs = [(7, 2), (7, 2), (2, 7), (6,), (7,)]
    sems = [dma(shape) for shape in pairs for _ in range(2)]
    return pl.pallas_call(
        fused_kernel,
        out_shape=jax.ShapeDtypeStruct((rows, width), bf16),
        in_specs=[vmem] * 7 + [hbm] * 3,
        out_specs=vmem,
        scratch_shapes=[
            pltpu.VMEM((1024, HEAD_DIM), bf16),
            pltpu.VMEM((512, HEAD_DIM), bf16),
            pltpu.VMEM((2, 8, 2, 2, 4, 128, 128), bf16),
            pltpu.VMEM((2, 4, 128, 128), bf16),
            pltpu.VMEM((1024, 2 * HEAD_DIM), single),
            pltpu.VMEM((1024, HEAD_DIM), single),
            pltpu.VMEM((512, HEAD_DIM), bf16),
            pltpu.VMEM((2, 8, 512, HEAD_DIM), bf16),
            pltpu.VMEM((8, 256, 256), bf16),
            pltpu.VMEM(gate.shape, bf16),
            pltpu.VMEM(up.shape, bf16),
            pltpu.VMEM(down.shape, bf16),
            pltpu.VMEM((1024, 512), bf16),
            pltpu.VMEM((512, 1024), bf16),
            pltpu.VMEM((512, 256), bf16),
            pltpu.VMEM((32, 2, 16, 256), bf16),
            pltpu.VMEM((8, 8, 2, 4, 16, 256), bf16),
            pltpu.VMEM((2, 128, 2048), bf16),
            pltpu.VMEM((32, 2, 16, 256), bf16),
            pltpu.VMEM((8, 2, 4, 16, 256), bf16),
            pltpu.VMEM((8, 8, 2, 64, 256), bf16),
            pltpu.VMEM((8, 2, 64, 256), bf16),
            pltpu.VMEM((2, 8, 2, 64, 256), bf16),
            pltpu.VMEM((2, 8, 64, 256), bf16),
            pltpu.VMEM((2, 8, 2, 64, 256), bf16),
            pltpu.VMEM((8, 2, 64, 256), bf16),
            pltpu.VMEM((8, 2, 16, 256), bf16),
        ]
        + sems
        + [dma((3,)), dma((2, 9)), dma((2, 9))]
        + [dma((len(CHUNKS), 9)) for _ in range(4)]
        + [dma((8, 4)) for _ in range(4)],
        compiler_params=pltpu.CompilerParams(
            collective_id=0, has_side_effects=True, vmem_limit_bytes=VMEM_BYTES
        ),
        cost_estimate=pl.CostEstimate(
            flops=15 * 10**9, bytes_accessed=10**7, transcendentals=512 * 16384 * 2
        ),
    )(q, k, v, out_weight, residual, gain, ids, gate, up, down)


def per_device(
    residual,
    query_vectors,
    key_vectors,
    value_vectors,
    out_weight,
    norm_gain,
    species,
    gate_weight,
    up_weight,
    down_weight,
):
    return layer(
        query_vectors, key_vectors, value_vectors, out_weight, residual, norm_gain.reshape(1, -1),
        species.reshape(1, -1), jnp.swapaxes(gate_weight, 1, 2), jnp.swapaxes(up_weight, 1, 2), down_weight,
    )


def solution(mesh):
    return jax.shard_map(
        per_device,
        mesh=mesh,
        in_specs=(
            P("ctx", "exp"),
            P("ctx", "exp"),
            P("ctx", "exp"),
            P("ctx", "exp"),
            P("exp", None),
            P(),
            P("ctx", None),
            P("ctx", None, "exp"),
            P("ctx", None, "exp"),
            P("ctx", "exp", None),
        ),
        out_specs=P("ctx", "exp"),
        check_vma=False,
    )
```

```python
import functools
import math

import jax
import jax.numpy as jnp
from jax import lax
from jax.experimental import pallas as pl
from jax.experimental.pallas import tpu as pltpu
from jax.sharding import PartitionSpec as P

HEAD_DIM = 128
BLK = 8
MOST = 2
EPSILON = 1e-06
EXP2_FACTOR = math.log2(math.e) / math.sqrt(HEAD_DIM)
VMEM_BYTES = 60 * 1024 * 1024
TILE_Q = 512
Z_ORDER = (0, 1, 7, 2, 6, 3, 5, 4)
CHUNKS = ((0, 1), (1, 2), (2, 3), (3, 4), (4, 5), (5, 6), (6, 7), (7, 8))
ORDER = (
    (0, 0), (0, 1), (0, 2), (1, 0), (0, 3), (10, 0), (0, 4), (1, 2), (0, 5), (1, 1),
    (1, 3), (10, 1), (2, 0), (0, 6), (10, 2), (1, 4), (2, 2), (10, 5), (3, 0), (1, 5),
    (2, 1), (2, 3), (10, 3), (0, 7), (4, 0), (5, 0), (1, 6), (3, 2), (4, 2), (2, 4),
    (3, 1), (3, 3), (10, 4), (2, 5), (5, 2), (6, 0), (4, 1), (5, 1), (4, 3), (10, 6),
    (2, 6), (7, 0), (3, 4), (1, 7), (10, 7), (4, 4), (5, 3), (6, 2), (6, 1), (3, 5),
    (4, 5), (2, 7), (8, 0), (5, 4), (3, 6), (5, 5), (7, 1), (6, 3), (4, 6), (8, 1),
    (3, 7), (6, 4), (5, 6), (4, 7), (5, 7), (7, 3), (8, 3), (7, 2), (6, 5), (7, 4),
    (7, 5), (9, 0), (8, 2), (6, 6), (9, 1), (8, 4), (9, 3), (6, 7), (8, 5), (7, 6),
    (8, 6), (9, 2), (7, 7), (9, 4), (8, 7), (9, 5), (9, 6), (9, 7),
)
MESH = pl.DeviceIdType.MESH


def remote(src, dst, send_sem, recv_sem, where):
    return pltpu.make_async_remote_copy(
        src_ref=src,
        dst_ref=dst,
        send_sem=send_sem,
        recv_sem=recv_sem,
        device_id=where,
        device_id_type=MESH,
    )


def greet(others):
    barrier = pltpu.get_barrier_semaphore()
    for where in others:
        pl.semaphore_signal(barrier, inc=1, device_id=where, device_id_type=MESH)


def f32(value):
    return value.astype(jnp.float32)


def fused_kernel(
    q_ref, k_ref, v_ref, wo_hbm, res_hbm, gain_ref, ids_ref, gate_hbm, up_hbm, down_hbm,
    out_ref,
    wo_ref, res_ref, qbuf, q_give, kv, kv_give, acc, top, o_send, att, wo_cols,
    gate, up, down, pack, unpack, stream, packed, agb, normed, back, fin,
    parts, ya, pp, hh, tt, yb, yc,
    r_ss, r_rs, l_ss, l_rs, s_ss, s_rs, x_ss, x_rs, wo_ss, wo_rs, w_sem, a1_ss, a1_rs,
    rd_ss, rd_rs, ag_ss, ag_rs, b_ss, b_rs, f_ss, f_rs,
):
    ctx = lax.axis_index("ctx")
    z, lane = ctx // 4, ctx % 4
    exp = lax.axis_index("exp")
    x, y = exp % 4, exp // 4
    bf16 = jnp.bfloat16

    def at(dx, dy):
        return ((y + dy) % 2) * 4 + (x + dx) % 4

    def ctx_at(dz, dl):
        return ((z + dz) % 8) * 4 + (lane + dl) % 4

    me = at(0, 0)
    ahead, behind, across = {"exp": at(1, 0)}, {"exp": at(3, 0)}, {"exp": at(0, 1)}
    right, left = {"ctx": ctx_at(1, 0)}, {"ctx": ctx_at(7, 0)}
    sibling = {"ctx": z * 4 + (lane // 2) * 2 + (lane + 1) % 2}
    partner = {"ctx": ctx_at(0, 2)}

    exp_peers = [(dx, dy) for dy in range(2) for dx in range(4) if dx or dy]
    peers = [{"ctx": ctx_at(dz, dl)} for dz in range(8) for dl in range(4) if dz or dl]
    peers += [{"exp": at(dx, dy)} for dx, dy in exp_peers]
    greet(peers)
    loads = [
        pltpu.make_async_copy(src, dst, w_sem.at[i])
        for i, (src, dst) in enumerate(((gate_hbm, gate), (up_hbm, up), (down_hbm, down)))
    ]
    early = [
        pltpu.make_async_copy(wo_hbm, wo_ref, w_sem.at[3]),
        pltpu.make_async_copy(res_hbm, res_ref, w_sem.at[4]),
    ]
    for load in early + loads:
        load.start()

    head, far_head = lane // 2, 1 - lane // 2
    mine = pl.ds(pl.multiple_of(head * HEAD_DIM, HEAD_DIM), HEAD_DIM)
    theirs = pl.ds(pl.multiple_of(far_head * HEAD_DIM, HEAD_DIM), HEAD_DIM)
    for place, cols in ((kv.at[0, 0, 0], mine), (kv_give, theirs)):
        for j in range(4):
            rows = slice(j * 128, (j + 1) * 128)
            place[0, j] = k_ref[rows, cols].T
            place[1, j] = v_ref[rows, cols]
    qbuf[0:512] = q_ref[:, mine]
    q_give[...] = q_ref[:, theirs]

    pl.semaphore_wait(pltpu.get_barrier_semaphore(), len(peers))

    def right_item(t):
        return 1 + t // 2, t % 2

    def left_item(t):
        return 7 - t // 2, t % 2 + t // 6

    def right_copy(t, p):
        slot, part = right_item(t)
        return remote(
            kv.at[0, slot - 1, part, p], kv.at[0, slot, part, p], r_ss.at[t, p], r_rs.at[t, p], right
        )

    def left_copy(t, p):
        slot, part = left_item(t)
        return remote(
            kv.at[0, (slot + 1) % 8, part, p],
            kv.at[0, slot, part, p],
            l_ss.at[t, p],
            l_rs.at[t, p],
            left,
        )

    def sibling_copy(way, t):
        slot, part = (right_item, left_item)[way](t)
        return remote(
            kv.at[0, slot, part], kv.at[1, slot, part], s_ss.at[way, t], s_rs.at[way, t], sibling
        )

    kv_copies = [
        remote(kv_give.at[p], kv.at[0, 0, 1, p], x_ss.at[p], x_rs.at[p], partner) for p in range(2)
    ]
    query_copy = remote(q_give, qbuf.at[pl.ds(512, 512)], x_ss.at[2], x_rs.at[2], partner)
    out_copy = remote(o_send, att.at[1, me], x_ss.at[3], x_rs.at[3], partner)
    near_copy = remote(kv.at[0, 0, 0], kv.at[1, 0, 0], x_ss.at[4], x_rs.at[4], sibling)
    far_copy = remote(kv.at[0, 0, 1], kv.at[1, 0, 1], x_ss.at[5], x_rs.at[5], sibling)
    for p in range(2):
        right_copy(0, p).start()
        left_copy(0, p).start()
        kv_copies[p].start()
    near_copy.start()
    query_copy.start()

    def wo_block(index):
        return pl.ds(pl.multiple_of(index * 256, 256), 256)

    def wo_copy(i):
        dx, dy = exp_peers[i]
        to = at(dx, dy)
        return remote(
            wo_ref.at[:, wo_block(to)], wo_cols.at[me], wo_ss.at[i], wo_rs.at[i], {"exp": to}
        )

    acc[...] = jnp.zeros_like(acc)
    top[...] = jnp.full_like(top, -1e30)
    ones = jnp.ones((512, HEAD_DIM), bf16)

    def attend(first, count, chunks):
        def one_tile(index, unused):
            rows = pl.ds(pl.multiple_of(first + index * TILE_Q, TILE_Q), TILE_Q)
            q = qbuf[rows, :]
            scores = [
                jnp.dot(
                    q,
                    jnp.concatenate([kv[kind, slot, part, 0, j] for j in range(4)], axis=1),
                    preferred_element_type=jnp.float32,
                )
                for kind, slot, part in chunks
            ]
            before = top[rows, :]
            best = functools.reduce(jnp.maximum, scores)
            best = jnp.maximum(best[:, :256], best[:, 256:])
            best = jnp.maximum(best[:, :128], best[:, 128:])
            now = jnp.maximum(before, jnp.max(best, axis=1, keepdims=True))
            top[rows, :] = now
            wide_now = jnp.concatenate([now] * 4, axis=1)
            total = None
            for s, (kind, slot, part) in zip(scores, chunks):
                weights = jnp.exp2((s - wide_now) * EXP2_FACTOR).astype(bf16)
                wide = jnp.concatenate([kv[kind, slot, part, 1].reshape(512, 128), ones], axis=1)
                term = jnp.dot(weights, wide, preferred_element_type=jnp.float32)
                total = term if total is None else total + term
            shrink = jnp.exp2((before - now) * EXP2_FACTOR)
            acc[rows, :] = acc[rows, :] * jnp.concatenate([shrink, shrink], axis=1) + total
            return unused

        lax.fori_loop(0, count // TILE_Q, one_tile, 0)

    attend(0, 512, [(0, 0, 0)])
    near_copy.wait_recv()
    attend(0, 512, [(1, 0, 0)])
    def counter(shape, dim):
        return lax.broadcasted_iota(jnp.int32, shape, dim)

    def flag(condition):
        return jnp.where(condition, 1.0, 0.0)

    ids = jnp.broadcast_to(f32(ids_ref[...]), (64, 64))
    ids_t = ids.T
    same = flag(ids == ids_t)
    before_row = flag(counter((64, 64), 0) < counter((64, 64), 1))
    before_col = flag(counter((64, 64), 1) < counter((64, 64), 0))
    slot_row = MOST * ids[0:1, :] + jnp.sum(same * before_row, axis=0, keepdims=True)
    slot_col = MOST * ids_t[:, 0:1] + jnp.sum(same * before_col, axis=1, keepdims=True)
    spans = flag(counter((64, 512), 1) // BLK == counter((64, 512), 0)).astype(bf16)
    spans_t = flag(counter((512, 64), 0) // BLK == counter((512, 64), 1)).astype(bf16)
    token_row = jnp.dot(
        jnp.broadcast_to(slot_row, (8, 64)).astype(bf16), spans, preferred_element_type=jnp.float32
    ).astype(jnp.int32)[0:1, :] * BLK + counter((1, 512), 1) % BLK
    token_col = jnp.dot(
        spans_t, jnp.broadcast_to(slot_col, (64, 128)).astype(bf16),
        preferred_element_type=jnp.float32,
    ).astype(jnp.int32) * BLK + counter((512, 128), 0) % BLK
    for part in range(4):
        places = counter((256, 512), 0) + part * 256
        pack[part * 256 : (part + 1) * 256, :] = flag(places == token_row).astype(bf16)
    for part in range(8):
        places = counter((512, 128), 1) + part * 128
        unpack[:, part * 128 : (part + 1) * 128] = flag(places == token_col).astype(bf16)
    for p in range(2):
        kv_copies[p].wait_recv()
        right_copy(1, p).start()
        left_copy(1, p).start()
    far_copy.start()
    attend(0, 512, [(0, 0, 1)])
    for load in early:
        load.wait()
    for i in range(7):
        wo_copy(i).start()
    wo_cols[me] = wo_ref[:, wo_block(me)]

    def pass_on(t):
        for p in range(2):
            right_copy(t, p).wait_recv()

            @pl.when(t < 5)
            def _():
                right_copy(t + 2, p).start()

            left_copy(t, p).wait_recv()

            @pl.when(t < 4)
            def _():
                left_copy(t + 2, p).start()

            @pl.when(t == 5)
            def _():
                left_copy(6, p).start()

        sibling_copy(0, t).start()
        sibling_copy(1, t).start()

    def stage(t, unused):
        pass_on(t)

        @pl.when(t == 0)
        def _():
            query_copy.wait_recv()
            far_copy.wait_recv()

        @pl.when(t < 5)
        def _():
            attend(512 * (1 - t // 4), 512, [(t % 2 + t // 4, 0, t // 2 - t // 4)])

        attend(0, 1024, [(0,) + right_item(t), (0,) + left_item(t)])
        sibling_copy(0, t).wait_recv()
        sibling_copy(1, t).wait_recv()
        attend(0, 1024, [(1,) + right_item(t), (1,) + left_item(t)])
        return unused

    lax.fori_loop(0, 6, stage, 0)

    def many(c, way):
        return pl.ds(128, 384) if c == way else pl.ds(0, 512)

    def spread_copy(c, i):
        low, high = pl.ds(0, 256), pl.ds(256, 256)
        src, where = (
            (att.at[c, me], across),
            (att.at[c, me], ahead),
            (att.at[c, me], behind),
            (att.at[c, at(0, 1), many(c, 0)], ahead),
            (att.at[c, at(0, 1), many(c, 1)], behind),
            (att.at[c, at(3, 0), low], ahead),
            (att.at[c, at(1, 0), high], behind),
            (att.at[c, at(2, 0)], across),
            (att.at[c, at(3 if c == 0 else 1, 0), pl.ds(0, 128)], across),
        )[i]
        return remote(src, src, a1_ss.at[c, i], a1_rs.at[c, i], where)

    def spread_landed(c, i):
        low, high = pl.ds(0, 256), pl.ds(256, 256)
        dst = (
            att.at[c, at(0, 1)],
            att.at[c, at(3, 0)],
            att.at[c, at(1, 0)],
            att.at[c, at(3, 1), many(c, 0)],
            att.at[c, at(1, 1), many(c, 1)],
            att.at[c, at(2, 0), low],
            att.at[c, at(2, 0), high],
            att.at[c, at(2, 1)],
            att.at[c, at(3 if c == 0 else 1, 1), pl.ds(0, 128)],
        )[i]
        remote(dst, dst, a1_ss.at[c, i], a1_rs.at[c, i], across).wait_recv()

    pass_on(6)
    attend(0, 512, [(0, 4, 0), (0, 4, 1)])
    sibling_copy(0, 6).wait_recv()
    sibling_copy(1, 6).wait_recv()
    attend(0, 512, [(1, 4, 0), (1, 4, 1)])
    att[0, me] = (acc[:512, :HEAD_DIM] / acc[:512, HEAD_DIM:]).astype(bf16)
    for i in range(3):
        spread_copy(0, i).start()
    attend(512, 512, [(0, 4, 0), (0, 4, 1)])
    attend(512, 512, [(1, 4, 0), (1, 4, 1)])
    o_send[...] = (acc[512:, :HEAD_DIM] / acc[512:, HEAD_DIM:]).astype(bf16)
    out_copy.start()
    for c in range(2):
        if c == 1:
            out_copy.wait_recv()
            for i in range(3):
                spread_copy(1, i).start()
        for i, nexts in ((1, (5,)), (2, (6, 8)), (0, (3, 4))):
            spread_landed(c, i)
            for n in nexts:
                spread_copy(c, n).start()
    for c in range(2):
        spread_landed(c, 5)
        spread_landed(c, 6)
        spread_copy(c, 7).start()
    for i in range(7):
        dx, dy = exp_peers[i]
        dst = wo_cols.at[at(4 - dx, dy)]
        remote(dst, dst, wo_ss.at[i], wo_rs.at[i], across).wait_recv()
    for c in range(2):
        for i in (3, 4, 7, 8):
            spread_landed(c, i)
    near_rows, far_rows = mine, theirs
    for part in range(2):
        rows = slice(part * 256, (part + 1) * 256)
        total = f32(res_ref[rows, :])
        for f in range(8):
            total = total + jnp.dot(
                jnp.concatenate([att[0, f, rows, :], att[1, f, rows, :]], axis=1),
                jnp.concatenate([wo_cols[f, near_rows, :], wo_cols[f, far_rows, :]], axis=0),
                preferred_element_type=jnp.float32,
            )
        stream[rows, :] = total.astype(bf16)

    slots = [(n, dl) for n in range(8) for dl in range(4)]

    def remote_slots(c):
        return [s for s in slots if s[0] in range(*CHUNKS[c]) and s != (0, 0)]

    def send_copy(n, dl):
        to = ctx_at(Z_ORDER[n], dl)
        return remote(
            packed.at[to], agb.at[me, n, :, dl], b_ss.at[n, dl], b_rs.at[n, dl], {"ctx": to}
        )

    def back_copy(n, dl):
        to = ctx_at(8 - Z_ORDER[n], 4 - dl)
        return remote(
            fin.at[n, :, dl], back.at[ctx], f_ss.at[n, dl], f_rs.at[n, dl], {"ctx": to}
        )

    for part in range(4):
        packed[part * 8 : (part + 1) * 8] = jnp.dot(
            pack[part * 256 : (part + 1) * 256, :], stream[...],
            preferred_element_type=jnp.float32,
        ).astype(bf16).reshape(8, 2, 16, 256)
    for c in range(len(CHUNKS)):
        for slot in remote_slots(c):
            send_copy(*slot).start()
    agb[me, 0, :, 0] = packed[ctx]

    def span(c):
        return pl.ds(CHUNKS[c][0], CHUNKS[c][1] - CHUNKS[c][0])

    def some(c, way):
        return pl.ds(1, 3) if c % 2 == way else pl.ds(0, 4)

    def some_rows(c, way):
        return pl.ds(16, 48) if c % 2 == way else pl.ds(0, 64)

    def gather_copy(c, i):
        rows = span(c)
        src, where = (
            (agb.at[me, rows], across),
            (agb.at[me, rows], ahead),
            (agb.at[me, rows], behind),
            (agb.at[at(0, 1), rows, :, some(c, 0)], ahead),
            (agb.at[at(0, 1), rows, :, some(c, 1)], behind),
            (agb.at[at(3, 0), rows, 0], ahead),
            (agb.at[at(1, 0), rows, 1], behind),
            (agb.at[at(2, 0), rows], across),
            (agb.at[at(3 if c % 2 == 0 else 1, 0), rows, :, pl.ds(0, 1)], across),
        )[i]
        return remote(src, src, ag_ss.at[c, i], ag_rs.at[c, i], where)

    def gather_first(c):
        for slot in remote_slots(c):
            send_copy(*slot).wait_recv()
        for i in range(3):
            gather_copy(c, i).start()

    def landed(c, i):
        rows = span(c)
        dst = (
            agb.at[at(0, 1), rows],
            agb.at[at(3, 0), rows],
            agb.at[at(1, 0), rows],
            agb.at[at(3, 1), rows, :, some(c, 0)],
            agb.at[at(1, 1), rows, :, some(c, 1)],
            agb.at[at(2, 0), rows, 0],
            agb.at[at(2, 0), rows, 1],
            agb.at[at(2, 1), rows],
            agb.at[at(3 if c % 2 == 0 else 1, 1), rows, :, pl.ds(0, 1)],
        )[i]
        remote(dst, dst, ag_ss.at[c, i], ag_rs.at[c, i], across).wait_recv()

    def gather_near(c):
        landed(c, 0)
        gather_copy(c, 3).start()
        gather_copy(c, 4).start()

    def gather_second(c):
        landed(c, 1)
        gather_copy(c, 5).start()
        landed(c, 2)
        gather_copy(c, 6).start()
        gather_copy(c, 8).start()

    def gather_third(c):
        landed(c, 5)
        landed(c, 6)
        gather_copy(c, 7).start()

    def gather_last(c):
        for i in (3, 4, 7, 8):
            landed(c, i)

    def sum_copy(c, i):
        rows = span(c)
        src, dst, where = (
            (parts.at[at(2, 1), rows], ya.at[rows], across),
            (parts.at[at(1, 1), rows, :, some_rows(c, 0)], pp.at[0, rows, :, some_rows(c, 0)], ahead),
            (parts.at[at(3, 1), rows, :, some_rows(c, 1)], pp.at[1, rows, :, some_rows(c, 1)], behind),
            (parts.at[at(2, 0), rows, 0], hh.at[0, rows], ahead),
            (parts.at[at(2, 0), rows, 1], hh.at[1, rows], behind),
            (parts.at[at(1, 0), rows], tt.at[0, rows], ahead),
            (parts.at[at(3, 0), rows], tt.at[1, rows], behind),
            (parts.at[at(0, 1), rows], yb.at[rows], across),
            (parts.at[at(1 if c % 2 == 0 else 3, 1), rows, :, pl.ds(0, 16)], yc.at[rows], across),
        )[i]
        return remote(src, dst, rd_ss.at[c, i], rd_rs.at[c, i], where)

    def sum_first(c):
        for i in (0, 1, 2, 8):
            sum_copy(c, i).start()

    def sum_second(c):
        rows = span(c)
        sum_copy(c, 0).wait_recv()
        far = at(2, 0)
        parts[far, rows] = (f32(parts[far, rows]) + f32(ya[rows])).astype(bf16)
        sum_copy(c, 3).start()
        sum_copy(c, 4).start()

    def sum_third(c):
        rows = span(c)
        sum_copy(c, 1).wait_recv()
        sum_copy(c, 2).wait_recv()
        other, short = at(0, 1), c % 2
        few, most = pl.ds(0, 16), pl.ds(16, 48)
        parts[other, rows, :, few] = (
            f32(parts[other, rows, :, few]) + f32(pp[1 - short, rows, :, few])
        ).astype(bf16)
        parts[other, rows, :, most] = (
            f32(parts[other, rows, :, most])
            + f32(pp[0, rows, :, most])
            + f32(pp[1, rows, :, most])
        ).astype(bf16)
        sum_copy(c, 7).start()

    def sum_fourth(c):
        rows, few = span(c), pl.ds(0, 16)
        sum_copy(c, 8).wait_recv()
        near = at(1 if c % 2 == 0 else 3, 0)
        parts[near, rows, :, few] = (f32(parts[near, rows, :, few]) + f32(yc[rows])).astype(bf16)
        for way in range(2):
            sum_copy(c, 3 + way).wait_recv()
            near = at(1 if way == 0 else 3, 0)
            parts[near, rows, way] = (f32(parts[near, rows, way]) + f32(hh[way, rows])).astype(bf16)
            sum_copy(c, 5 + way).start()

    def sum_last(c):
        rows = span(c)
        for i in (5, 6, 7):
            sum_copy(c, i).wait_recv()
        return (f32(parts[me, rows]) + f32(tt[0, rows])) + (f32(tt[1, rows]) + f32(yb[rows]))

    def experts(c):
        rows = span(c)
        count = CHUNKS[c][1] - CHUNKS[c][0]
        height = count * 64
        for e in range(2):
            square = jnp.zeros((height, 1), jnp.float32)
            for f in range(8):
                piece = f32(agb[f, rows, e].reshape(height, 256))
                square = square + jnp.sum(piece * piece, axis=1, keepdims=True)
            scale = lax.rsqrt(square * (1.0 / 2048) + EPSILON)
            for f in range(8):
                cols = slice(f * 256, (f + 1) * 256)
                piece = f32(agb[f, rows, e].reshape(height, 256))
                normed[e, :height, cols] = (piece * scale * gain_ref[:, cols]).astype(bf16)
            lifted = lax.dot_general(
                normed[e, :height, :], up[e], (((1,), (1,)), ((), ())),
                preferred_element_type=jnp.float32,
            )
            gated = lax.dot_general(
                normed[e, :height, :], gate[e], (((1,), (1,)), ((), ())),
                preferred_element_type=jnp.float32,
            )
            hidden = (gated / (1.0 + jnp.exp(-gated)) * lifted).astype(bf16)
            for f in range(8):
                parts[f, rows, e] = jnp.dot(
                    hidden, down[e, :, f * 256 : (f + 1) * 256],
                    preferred_element_type=jnp.float32,
                ).astype(bf16).reshape(count, 64, 256)

    def finish(c):
        rows = span(c)
        count = CHUNKS[c][1] - CHUNKS[c][0]
        fin[rows] = sum_last(c).astype(bf16).reshape(count, 2, 4, 16, 256)
        for slot in remote_slots(c):
            back_copy(*slot).start()
        if c == 0:
            back[ctx] = fin[0, :, 0]

    steps = (
        gather_first, gather_second, gather_third, gather_last, experts,
        sum_first, sum_second, sum_third, sum_fourth, finish, gather_near,
    )
    ready = False
    for step, c in ORDER:
        if steps[step] is experts and not ready:
            for load in loads:
                load.wait()
            ready = True
        steps[step](c)

    for n, dl in slots[1:]:
        dst = back.at[ctx_at(Z_ORDER[n], dl)]
        remote(dst, dst, f_ss.at[n, dl], f_rs.at[n, dl], across).wait_recv()
    for rows in (slice(0, 256), slice(256, 512)):
        moved = jnp.dot(
            unpack[rows, :], back[...].reshape(1024, 256), preferred_element_type=jnp.float32
        )
        out_ref[rows, :] = (f32(stream[rows, :]) + moved).astype(bf16)

    def drain(t, unused):
        for p in range(2):
            right_copy(t, p).wait_send()
            left_copy(t, p).wait_send()
        sibling_copy(0, t).wait_send()
        sibling_copy(1, t).wait_send()
        return unused

    lax.fori_loop(0, 7, drain, 0)
    for copy in kv_copies + [query_copy, out_copy, near_copy, far_copy]:
        copy.wait_send()
    for i in range(7):
        wo_copy(i).wait_send()
    for c in range(2):
        for i in range(9):
            spread_copy(c, i).wait_send()
    for c in range(len(CHUNKS)):
        for i in range(9):
            sum_copy(c, i).wait_send()
            gather_copy(c, i).wait_send()
    for slot in slots[1:]:
        send_copy(*slot).wait_send()
        back_copy(*slot).wait_send()


def layer(q, k, v, out_weight, residual, gain, ids, gate, up, down):
    rows, width = residual.shape
    dma = pltpu.SemaphoreType.DMA
    vmem, hbm = pl.BlockSpec(memory_space=pltpu.VMEM), pl.BlockSpec(memory_space=pl.ANY)
    bf16, single = jnp.bfloat16, jnp.float32
    pairs = [(7, 2), (7, 2), (2, 7), (6,), (7,)]
    sems = [dma(shape) for shape in pairs for _ in range(2)]
    return pl.pallas_call(
        fused_kernel,
        out_shape=jax.ShapeDtypeStruct((rows, width), bf16),
        in_specs=[vmem] * 3 + [hbm] * 2 + [vmem] * 2 + [hbm] * 3,
        out_specs=vmem,
        scratch_shapes=[
            pltpu.VMEM(out_weight.shape, bf16),
            pltpu.VMEM(residual.shape, bf16),
            pltpu.VMEM((1024, HEAD_DIM), bf16),
            pltpu.VMEM((512, HEAD_DIM), bf16),
            pltpu.VMEM((2, 8, 2, 2, 4, 128, 128), bf16),
            pltpu.VMEM((2, 4, 128, 128), bf16),
            pltpu.VMEM((1024, 2 * HEAD_DIM), single),
            pltpu.VMEM((1024, HEAD_DIM), single),
            pltpu.VMEM((512, HEAD_DIM), bf16),
            pltpu.VMEM((2, 8, 512, HEAD_DIM), bf16),
            pltpu.VMEM((8, 256, 256), bf16),
            pltpu.VMEM(gate.shape, bf16),
            pltpu.VMEM(up.shape, bf16),
            pltpu.VMEM(down.shape, bf16),
            pltpu.VMEM((1024, 512), bf16),
            pltpu.VMEM((512, 1024), bf16),
            pltpu.VMEM((512, 256), bf16),
            pltpu.VMEM((32, 2, 16, 256), bf16),
            pltpu.VMEM((8, 8, 2, 4, 16, 256), bf16),
            pltpu.VMEM((2, 128, 2048), bf16),
            pltpu.VMEM((32, 2, 16, 256), bf16),
            pltpu.VMEM((8, 2, 4, 16, 256), bf16),
            pltpu.VMEM((8, 8, 2, 64, 256), bf16),
            pltpu.VMEM((8, 2, 64, 256), bf16),
            pltpu.VMEM((2, 8, 2, 64, 256), bf16),
            pltpu.VMEM((2, 8, 64, 256), bf16),
            pltpu.VMEM((2, 8, 2, 64, 256), bf16),
            pltpu.VMEM((8, 2, 64, 256), bf16),
            pltpu.VMEM((8, 2, 16, 256), bf16),
        ]
        + sems
        + [dma((5,)), dma((2, 9)), dma((2, 9))]
        + [dma((len(CHUNKS), 9)) for _ in range(4)]
        + [dma((8, 4)) for _ in range(4)],
        compiler_params=pltpu.CompilerParams(
            collective_id=0, has_side_effects=True, vmem_limit_bytes=VMEM_BYTES
        ),
        cost_estimate=pl.CostEstimate(
            flops=15 * 10**9, bytes_accessed=10**7, transcendentals=512 * 16384 * 2
        ),
    )(q, k, v, out_weight, residual, gain, ids, gate, up, down)


def per_device(
    residual,
    query_vectors,
    key_vectors,
    value_vectors,
    out_weight,
    norm_gain,
    species,
    gate_weight,
    up_weight,
    down_weight,
):
    return layer(
        query_vectors, key_vectors, value_vectors, out_weight, residual, norm_gain.reshape(1, -1),
        species.reshape(1, -1), jnp.swapaxes(gate_weight, 1, 2), jnp.swapaxes(up_weight, 1, 2), down_weight,
    )


def solution(mesh):
    return jax.shard_map(
        per_device,
        mesh=mesh,
        in_specs=(
            P("ctx", "exp"),
            P("ctx", "exp"),
            P("ctx", "exp"),
            P("ctx", "exp"),
            P("exp", None),
            P(),
            P("ctx", None),
            P("ctx", None, "exp"),
            P("ctx", None, "exp"),
            P("ctx", "exp", None),
        ),
        out_specs=P("ctx", "exp"),
        check_vma=False,
    )
```
